512 devices in a mesh: dp: 128 (over x_lo, z, y), head: 4 (over x_hi, core).
Axes of the slice: x: 4 (x_hi: 2, x_lo: 2; x = x_hi * 2 + x_lo), y: 4, z: 16, core: 2. Of those that a mesh axis runs over, the one named last changes fastest.
Arguments:
- prompt_kv: bfloat16 [2, 4096, 128], P(None, 'dp', 'head'), may hold values from -6 to 6
- resp_kv: bfloat16 [2, 49152, 128], P(None, 'dp', 'head'), may hold values from -6 to 6
- resp_query: bfloat16 [49152, 512], P('dp', 'head'), may hold values from -240 to 240
- resp_out: bfloat16 [49152, 512], P('dp', 'head'), may hold values from -6 to 6
- resp_dout: bfloat16 [49152, 512], P('dp', 'head'), may hold values from -6 to 6
- resp_lengths: int32 [4, 16], replicated, may hold values from 1 to 1536, 12288 in all within a row
- prompt_owner: int32 [128], replicated, may hold values from 0 to 127, each once
Outputs:
- query_grad: bfloat16 [49152, 512], P('dp', 'head')
- resp_kv_grad: bfloat16 [2, 49152, 128], P(None, 'dp', 'head')
- prompt_kv_grad: bfloat16 [2, 4096, 128], P(None, 'dp', 'head')
The draws below stay inside these ranges and needn't reach their ends.
Inputs may be any that keep to these rules, and one draw needn't show every extreme that they name: `resp_lengths`: each group's lengths sum to 12288; the longest is 1536. `prompt_owner`: each piece number appears once.
All inputs are finite; a program needn't handle non-finite values.
Results may differ from the reference program's by a relative error of at most 0.018.
Values may be sent and summed in bfloat16 or wider, within the bound.
No kernel may reach another device: no remote copies, remote signals or barrier semaphores. Data moves between devices by JAX's collectives and lax.ppermute only.
A program may use at most 64 MiB of HBM per device.

```python
import math
import jax
import jax.numpy as jnp
import numpy as np
from jax import lax

HD = 128
HQ = 4
NGRP = 4
PROWS = 32
RROWS = 384
PSH = 32
PLEN = 1024
NRESP = 16
MAXLEN = 1536
HOPS = 4
NSHARD = 128
RTOT = 49152
PTOT = 4096


def draw_resp_query(key, part):
    key = jax.random.fold_in(key, 7)
    base = jnp.clip(jax.random.normal(key, (RTOT, HQ * HD), jnp.float32), -6.0, 6.0)
    return base.astype(jnp.bfloat16)


def levels(stream_key, dims, shards, low, top_value):
    def one(position, shards_of):
        steps = jax.random.uniform(jax.random.fold_in(jax.random.fold_in(stream_key, 6), position), (shards_of,), jnp.float32, low / len(shards), top_value / len(shards))
        return jnp.repeat(jnp.exp(steps), dims[position] // shards_of).reshape((-1,) + (1,) * (len(dims) - position - 1))

    factor_of = one(*shards[0])
    for cut in shards[1:]:
        factor_of = factor_of * one(*cut)
    return factor_of


def split_up(number_of, total, limit, skew):
    weights = [(1 << 20) // math.isqrt(standing ** skew) + 1 for standing in range(2, number_of + 1)]
    surplus, holding = total - limit - (number_of - 1), [1] * (number_of - 1)
    while surplus > 0:
        movable = [i for i in range(number_of - 1) if holding[i] < limit]
        whole, left = sum([weights[i] for i in movable]), surplus
        for i in movable:
            more = min(limit - holding[i], max(1, left * weights[i] // whole), surplus)
            holding[i] = holding[i] + more
            surplus = surplus - more
    return np.array([limit] + holding)


def uneven_parts(stream_key, count, total, limit, slope):
    if count == 2:
        one = jax.random.randint(stream_key, (), max(1, total - limit), min(limit, total - 1) + 1)
        return jnp.stack([one, total - one])
    sizes = jnp.asarray(split_up(count, total, limit, slope), jnp.int32)
    pairs = (count - 1) // 2
    giver, sink = sizes[1:1 + 2 * pairs:2], sizes[2:2 + 2 * pairs:2]
    slack = jnp.minimum(giver - 1, limit - sink)
    moved = jax.random.randint(jax.random.fold_in(stream_key, 1), (pairs,), 0, 1 << 20) % (slack + 1)
    sizes = sizes.at[1:1 + 2 * pairs:2].set(giver - moved).at[2:2 + 2 * pairs:2].set(sink + moved)
    return sizes[jax.random.permutation(jax.random.fold_in(stream_key, 2), count)]


def bell_draw(own_key, extent, spread, most, split=(), held_as=jnp.bfloat16):
    array = spread * jax.random.normal(own_key, extent, jnp.float32)
    if split:
        array = array * levels(own_key, extent, split, -0.22, 0.18)
    return jnp.clip(array, -most, most).astype(held_as)


def setup_inputs(seed: int = 0) -> dict:
    arg_keys = jax.random.split(jax.random.key(seed), 8)
    prompt_kv = bell_draw(arg_keys[0], (2, PTOT, HD), 1.0, 6.0, ((1, 128), (2, 4)))
    resp_kv = bell_draw(arg_keys[1], (2, RTOT, HD), 1.0, 6.0, ((1, 128), (2, 4)))
    resp_query = draw_resp_query(jax.random.fold_in(arg_keys[7], 71), 0)
    resp_out = bell_draw(arg_keys[3], (RTOT, HQ * HD), 1.0, 6.0, ((0, 128), (1, 4)))
    resp_dout = bell_draw(arg_keys[4], (RTOT, HQ * HD), 1.0, 6.0, ((0, 128), (1, 4)))
    resp_lengths = jax.vmap(lambda own: uneven_parts(own, NRESP, PSH * RROWS, MAXLEN, 2))(jax.random.split(arg_keys[5], NGRP)).reshape((NGRP, NRESP)).astype(jnp.int32)
    prompt_owner = jax.random.permutation(arg_keys[6], NSHARD).astype(jnp.int32)
    return dict(prompt_kv=prompt_kv, resp_kv=resp_kv, resp_query=resp_query, resp_out=resp_out, resp_dout=resp_dout, resp_lengths=resp_lengths, prompt_owner=prompt_owner)


def response_ids(row_index, lengths, per_group):
    row_group = row_index // per_group
    offset = row_index % per_group
    bounds = jnp.cumsum(lengths, axis=1).astype(jnp.int32)
    group_count = lengths.shape[0]
    resp_count = lengths.shape[1]
    chosen = row_group[:, None] == jnp.arange(group_count, dtype=jnp.int32)[None, :]
    passed = offset[:, None, None] >= bounds[None, :, :]
    finished = jnp.sum(jnp.where(chosen[:, :, None] & passed, 1, 0), axis=(1, 2)).astype(jnp.int32)
    resp_index = (row_group * resp_count + finished).astype(jnp.int32)
    return jnp.where(row_index >= 0, resp_index, -1).astype(jnp.int32)


def attend_block(queries, dout, saved_out, group_kv, local_kv, allowed, factor):
    queries_f = queries.astype(jnp.float32)
    dout_f = dout.astype(jnp.float32)
    prompt_keys = group_kv[0].astype(jnp.float32)
    prompt_values = group_kv[1].astype(jnp.float32)
    local_keys = local_kv[0].astype(jnp.float32)
    local_values = local_kv[1].astype(jnp.float32)
    prompt_scores = jnp.einsum('rhd,pd->hrp', queries_f, prompt_keys) * factor
    local_scores = jnp.einsum('rhd,ld->hrl', queries_f, local_keys) * factor
    local_scores = jnp.where(allowed[None], local_scores, -jnp.inf)
    row_max = jnp.maximum(jnp.max(prompt_scores, -1), jnp.max(local_scores, -1))
    row_sum = jnp.sum(jnp.exp(prompt_scores - row_max[..., None]), -1) + jnp.sum(jnp.exp(local_scores - row_max[..., None]), -1)
    log_total = row_max + jnp.log(row_sum)
    prompt_probs = jnp.exp(prompt_scores - log_total[..., None])
    local_probs = jnp.exp(local_scores - log_total[..., None])
    row_dot = jnp.sum(dout_f * saved_out.astype(jnp.float32), -1).T
    prompt_dp = jnp.einsum('rhd,pd->hrp', dout_f, prompt_values)
    local_dp = jnp.einsum('rhd,ld->hrl', dout_f, local_values)
    prompt_ds = (prompt_probs * (prompt_dp - row_dot[..., None])).astype(jnp.bfloat16).astype(jnp.float32)
    local_ds = (local_probs * (local_dp - row_dot[..., None])).astype(jnp.bfloat16).astype(jnp.float32)
    prompt_pb = prompt_probs.astype(jnp.bfloat16).astype(jnp.float32)
    local_pb = local_probs.astype(jnp.bfloat16).astype(jnp.float32)
    query_sums = (jnp.einsum('hrp,pd->rhd', prompt_ds, prompt_keys) + jnp.einsum('hrl,ld->rhd', local_ds, local_keys)) * factor
    prompt_terms = jnp.stack([jnp.einsum('hrp,rhd->pd', prompt_ds, queries_f) * factor, jnp.einsum('hrp,rhd->pd', prompt_pb, dout_f)])
    local_terms = jnp.stack([jnp.einsum('hrl,rhd->ld', local_ds, queries_f) * factor, jnp.einsum('hrl,rhd->ld', local_pb, dout_f)])
    return query_sums, prompt_terms, local_terms


def reference(prompt_kv, resp_kv, resp_query, resp_out, resp_dout, resp_lengths, prompt_owner):
    factor = HD ** -0.5
    per_group = PSH * RROWS
    block_count = RTOT // RROWS
    holders = jnp.stack([jnp.nonzero(prompt_owner // PSH == gg, size=PSH)[0].astype(jnp.int32) for gg in range(NGRP)])
    picked_all = (holders[:, :, None] * PROWS + jnp.arange(PROWS, dtype=jnp.int32)[None, None, :]).reshape(NGRP, PLEN).astype(jnp.int32)
    padded = jnp.concatenate([jnp.zeros((2, HOPS * RROWS, HD), resp_kv.dtype), resp_kv], axis=1)

    def one_block(block):
        block_group = block // PSH
        picked = lax.dynamic_index_in_dim(picked_all, block_group, 0, keepdims=False)
        group_kv = jnp.take(prompt_kv, picked, axis=1)
        start = (block * RROWS).astype(jnp.int32)
        local_kv = lax.dynamic_slice_in_dim(padded, start, (HOPS + 1) * RROWS, 1)
        queries = lax.dynamic_slice_in_dim(resp_query, start, RROWS, 0).reshape(RROWS, HQ, HD)
        dout = lax.dynamic_slice_in_dim(resp_dout, start, RROWS, 0).reshape(RROWS, HQ, HD)
        saved_out = lax.dynamic_slice_in_dim(resp_out, start, RROWS, 0).reshape(RROWS, HQ, HD)
        query_rows = start + jnp.arange(RROWS, dtype=jnp.int32)
        key_rows = start - HOPS * RROWS + jnp.arange((HOPS + 1) * RROWS, dtype=jnp.int32)
        query_ids = response_ids(query_rows, resp_lengths, per_group)
        key_ids = response_ids(key_rows, resp_lengths, per_group)
        allowed = (query_ids[:, None] == key_ids[None, :]) & (key_rows[None, :] <= query_rows[:, None])
        return attend_block(queries, dout, saved_out, group_kv, local_kv, allowed, factor)

    query_sums, prompt_terms, local_terms = lax.map(one_block, jnp.arange(block_count, dtype=jnp.int32))
    query_grad = query_sums.reshape(RTOT, HQ * HD).astype(jnp.bfloat16)
    resp_sum = local_terms[:, :, HOPS * RROWS:]
    for distance in range(1, HOPS + 1):
        piece = local_terms[distance:, :, (HOPS - distance) * RROWS:(HOPS - distance + 1) * RROWS]
        resp_sum = resp_sum + jnp.concatenate([piece, jnp.zeros((distance, 2, RROWS, HD), jnp.float32)], axis=0)
    resp_total = jnp.transpose(resp_sum, (1, 0, 2, 3)).reshape(2, RTOT, HD)
    group_sums = jnp.sum(prompt_terms.reshape(NGRP, PSH, 2, PLEN, HD), axis=1)
    group_sums = jnp.transpose(group_sums, (1, 0, 2, 3)).reshape(2, NGRP * PLEN, HD)
    prompt_total = jnp.zeros((2, PTOT, HD), jnp.float32).at[:, picked_all.reshape(-1)].set(group_sums)
    return query_grad, resp_total.astype(jnp.bfloat16), prompt_total.astype(jnp.bfloat16)
```

```python
import jax
import jax.numpy as jnp
from jax import lax
from jax.sharding import PartitionSpec as P


def shifted(array, axis, by):
    size = lax.axis_size(axis)
    pairs = [(i, i + by) for i in range(size) if 0 <= i + by < size]
    return lax.ppermute(array, axis, pairs)


EXCHANGE_BITS = (32, 16, 8, 4, 2, 1, 64)


def doubled(array, axis, bits):
    size = lax.axis_size(axis)
    for bit in bits:
        other = lax.ppermute(array, axis, [(i, i ^ bit) for i in range(size)])
        array = jnp.concatenate([array, other], axis=0)
    return array


def slot_offsets(bits):
    slots = jnp.arange(1 << len(bits), dtype=jnp.int32)
    offsets = jnp.zeros_like(slots)
    for place, bit in enumerate(bits):
        offsets = offsets + ((slots >> place) & 1) * bit
    return offsets


def head_summed(terms):
    landed = lax.all_to_all(terms, "head", split_axis=0, concat_axis=0, tiled=True)
    return jnp.sum(landed.astype(jnp.float32), axis=0)


def response_ids(row_index, lengths, per_group):
    row_group = row_index // per_group
    offset = row_index % per_group
    bounds = jnp.cumsum(lengths, axis=1)
    group_count = lengths.shape[0]
    resp_count = lengths.shape[1]
    chosen = row_group[:, None] == jnp.arange(group_count, dtype=jnp.int32)[None, :]
    passed = offset[:, None, None] >= bounds[None, :, :]
    finished = jnp.sum(jnp.where(chosen[:, :, None] & passed, 1, 0), axis=(1, 2)).astype(jnp.int32)
    resp_index = row_group * resp_count + finished
    return jnp.where(row_index >= 0, resp_index, -1)


def score_block(queries, keys, allowed, factor):
    scores = jnp.einsum("rhd,pd->hrp", queries, keys, preferred_element_type=jnp.float32) * factor
    if allowed is None:
        return scores
    return jnp.where(allowed[None], scores, -jnp.inf)


def grad_block(queries, dout, row_dot, log_total, block_kv, allowed, factor):
    scores = score_block(queries, block_kv[0], allowed, factor)
    probs = jnp.exp(scores - log_total[..., None])
    value_dot = jnp.einsum("rhd,pd->hrp", dout, block_kv[1], preferred_element_type=jnp.float32)
    score_grad = (probs * (value_dot - row_dot[..., None])).astype(jnp.bfloat16)
    rounded = probs.astype(jnp.bfloat16)
    query_part = jnp.einsum(
        "hrp,pd->rhd", score_grad, block_kv[0], preferred_element_type=jnp.float32
    )
    key_terms = jnp.stack(
        [
            jnp.einsum("hrp,rhd->pd", score_grad, queries, preferred_element_type=jnp.float32)
            * factor,
            jnp.einsum("hrp,rhd->pd", rounded, dout, preferred_element_type=jnp.float32),
        ]
    )
    return (query_part, key_terms)


def body(prompt_kv, resp_kv, resp_query, resp_out, resp_dout, resp_lengths, prompt_owner):
    dp_devices = lax.axis_size("dp")
    own_index = lax.axis_index("dp")
    prompt_rows = prompt_kv.shape[1]
    resp_rows = resp_kv.shape[1]
    group_total = resp_lengths.shape[0]
    pieces_per_group = dp_devices // group_total
    reach_count = min(4, pieces_per_group - 1)
    own_group = own_index // pieces_per_group
    resp_full = lax.all_gather(resp_kv, "head", axis=2, tiled=True)
    head_size = lax.axis_size("head")
    narrow_width = prompt_kv.shape[2]
    head_width = resp_full.shape[2]
    factor = head_width ** (-0.5)
    pieces = doubled(prompt_kv.reshape(1, -1, 128), "dp", EXCHANGE_BITS)
    slot_holder = own_index ^ slot_offsets(EXCHANGE_BITS)
    all_holders = jnp.arange(dp_devices, dtype=jnp.int32)
    slot_piece = jnp.sum(
        jnp.where(slot_holder[:, None] == all_holders[None, :], prompt_owner[None, :], 0), axis=1
    )
    own_pieces = own_group * pieces_per_group + jnp.arange(pieces_per_group, dtype=jnp.int32)
    pick = (own_pieces[:, None] == slot_piece[None, :]).astype(jnp.bfloat16)
    group_pieces = jnp.dot(
        pick, pieces.reshape(dp_devices, -1), preferred_element_type=jnp.float32
    ).astype(jnp.bfloat16)
    gathered = lax.all_gather(group_pieces.reshape(-1, 128), "head", axis=0, tiled=False)
    group_kv = (
        gathered.reshape(head_size, pieces_per_group, 2, prompt_rows, narrow_width)
        .transpose(2, 1, 3, 0, 4)
        .reshape(2, pieces_per_group * prompt_rows, head_width)
    )
    sources = [resp_full]
    for distance in range(1, reach_count + 1):
        sources.append(shifted(resp_full, "dp", distance))
    first_row = own_index * resp_rows
    query_rows = first_row + jnp.arange(resp_rows, dtype=jnp.int32)
    per_group = pieces_per_group * resp_rows
    query_ids = response_ids(query_rows, resp_lengths, per_group)
    masks = []
    for distance in range(reach_count + 1):
        key_rows = first_row - distance * resp_rows + jnp.arange(resp_rows, dtype=jnp.int32)
        key_ids = response_ids(key_rows, resp_lengths, per_group)
        masks.append(
            (query_ids[:, None] == key_ids[None, :]) & (key_rows[None, :] <= query_rows[:, None])
        )
    head_count = resp_query.shape[1] // head_width
    queries = resp_query.reshape(resp_rows, head_count, head_width)
    dout = resp_dout.reshape(resp_rows, head_count, head_width)
    saved_out = resp_out.reshape(resp_rows, head_count, head_width)
    prompt_scores = score_block(queries, group_kv[0], None, factor)
    row_max = jnp.max(prompt_scores, -1)
    row_sum = jnp.sum(jnp.exp(prompt_scores - row_max[..., None]), -1)
    for distance in range(reach_count + 1):
        scores = score_block(queries, sources[distance][0], masks[distance], factor)
        new_max = jnp.maximum(row_max, jnp.max(scores, -1))
        row_sum = row_sum * jnp.exp(row_max - new_max) + jnp.sum(
            jnp.exp(scores - new_max[..., None]), -1
        )
        row_max = new_max
    log_total = row_max + jnp.log(row_sum)
    row_dot = jnp.sum(dout.astype(jnp.float32) * saved_out.astype(jnp.float32), -1).T
    query_sums, prompt_terms = grad_block(queries, dout, row_dot, log_total, group_kv, None, factor)
    local_terms = []
    for distance in range(reach_count + 1):
        query_part, key_terms = grad_block(
            queries, dout, row_dot, log_total, sources[distance], masks[distance], factor
        )
        query_sums = query_sums + query_part
        local_terms.append(key_terms)
    query_grad = (
        (query_sums * factor).reshape(resp_rows, head_count * head_width).astype(jnp.bfloat16)
    )
    own_terms = local_terms[0]
    for distance in range(1, reach_count + 1):
        own_terms = own_terms + shifted(
            local_terms[distance].astype(jnp.bfloat16), "dp", -distance
        ).astype(jnp.float32)
    resp_grad = head_summed(
        own_terms.astype(jnp.bfloat16)
        .reshape(2, resp_rows, head_size, narrow_width)
        .transpose(2, 0, 1, 3)
        .reshape(head_size, -1, 128)
    ).reshape(2, resp_rows, narrow_width)
    narrow = head_summed(
        prompt_terms.astype(jnp.bfloat16)
        .reshape(2, pieces_per_group, prompt_rows, head_size, narrow_width)
        .transpose(3, 1, 0, 2, 4)
        .reshape(head_size, -1, 128)
    ).astype(jnp.bfloat16)
    place = (prompt_owner[:, None] == own_pieces[None, :]).astype(jnp.bfloat16)
    spread = jnp.dot(
        place, narrow.reshape(pieces_per_group, -1), preferred_element_type=jnp.float32
    ).astype(jnp.bfloat16)
    landed = lax.all_to_all(
        spread.reshape(dp_devices, -1, 128), "dp", split_axis=0, concat_axis=0, tiled=True
    )
    prompt_grad = jnp.sum(landed.astype(jnp.float32), axis=0).reshape(
        2, prompt_rows, narrow_width
    )
    return (query_grad, resp_grad.astype(jnp.bfloat16), prompt_grad.astype(jnp.bfloat16))


def solution(mesh):
    in_specs = (
        P(None, "dp", "head"),
        P(None, "dp", "head"),
        P("dp", "head"),
        P("dp", "head"),
        P("dp", "head"),
        P(),
        P(),
    )
    out_specs = (P("dp", "head"), P(None, "dp", "head"), P(None, "dp", "head"))
    return jax.shard_map(body, mesh=mesh, in_specs=in_specs, out_specs=out_specs, check_vma=False)
```

```python
import jax
import jax.numpy as jnp
import numpy as np
from jax import lax
from jax.experimental import pallas as pl
from jax.experimental.pallas import tpu as pltpu
from jax.sharding import Mesh
from jax.sharding import PartitionSpec as P

XLO, Z, Y, HEADS = 2, 16, 4, 4
DP = XLO * Z * Y
WIDTH = 128
PART = WIDTH // HEADS
PIECES = 32
PROWS = 32
TILE = 2 * PROWS * PART // WIDTH
RROWS = 384
HOPS = 4
PROMPT = PIECES * PROWS
PACKED = 2 * RROWS * PART // WIDTH
QUARTER = PROMPT // HEADS
FACTOR = WIDTH**-0.5
LOG2E = 1.4426950408889634
VMEM = pl.BlockSpec(memory_space=pltpu.VMEM)
SMEM = pl.BlockSpec(memory_space=pltpu.SMEM)
PARAMS = pltpu.CompilerParams(vmem_limit_bytes=32 * 1024 * 1024)


def swap_matrix():
    shape = (HEADS * WIDTH, HEADS * WIDTH)
    row = lax.broadcasted_iota(jnp.int32, shape, 0)
    col = lax.broadcasted_iota(jnp.int32, shape, 1)
    target = ((row >> 5) & 3) * WIDTH + (row >> 7) * PART + (row & 31)
    return jnp.where(target == col, 1.0, 0.0).astype(jnp.bfloat16)


def swapped(rows, swap):
    return jnp.dot(rows, swap, preferred_element_type=jnp.float32)


def select_kernel(slots, pieces, picked):
    for piece in range(PIECES):
        picked[piece] = pieces[slots[piece]]


def place_kernel(slots, landed, spread, own):
    spread[...] = jnp.zeros_like(spread)
    total = landed[0].astype(jnp.float32)
    for head in range(1, HEADS):
        total = total + landed[head].astype(jnp.float32)
    rounded = total[: PIECES * TILE].astype(jnp.bfloat16)
    for piece in range(PIECES):
        spread[slots[piece]] = rounded[piece * TILE : (piece + 1) * TILE]
    own[...] = total[PIECES * TILE :]


def attention_kernel(
    place, q, o, do, start, prompt, near0, near1, near2, near3, near4, dq, close, far, exps, keys, values
):
    swap = swap_matrix()
    columns = swapped(jnp.concatenate([prompt[c] for c in range(HEADS)], axis=1), swap)
    for quarter in range(HEADS):
        part = columns[:, quarter * WIDTH : (quarter + 1) * WIDTH].reshape(PIECES, 2, TILE // 2, WIDTH)
        rows = slice(quarter * QUARTER, (quarter + 1) * QUARTER)
        keys[rows] = part[:, 0].reshape(QUARTER, WIDTH).astype(jnp.bfloat16)
        values[rows] = part[:, 1].reshape(QUARTER, WIDTH).astype(jnp.bfloat16)
    for distance, near in enumerate((near0, near1, near2, near3, near4)):
        rows = slice(PROMPT + distance * RROWS, PROMPT + (distance + 1) * RROWS)
        keys[rows] = near[0].T
        values[rows] = near[1].T
    chunks = [(i * QUARTER, QUARTER, None) for i in range(HEADS)]
    chunks += [(PROMPT + d * RROWS, RROWS, d) for d in range(HOPS + 1)]
    queries, dout = q[...], do[...]
    queries_t, dout_t = queries.T, dout.T
    products = dout.astype(jnp.float32) * o[...].astype(jnp.float32)
    delta = jnp.sum(products.T, axis=0, keepdims=True)
    first = start[...]
    peak = jnp.full((1, RROWS), -jnp.inf, jnp.float32)
    for begin, count, distance in chunks:
        rows = slice(begin, begin + count)
        scores = jnp.dot(keys[rows], queries_t, preferred_element_type=jnp.float32) * (FACTOR * LOG2E)
        if distance is not None:
            at = lax.broadcasted_iota(jnp.int32, (count, RROWS), 0) - distance * RROWS
            allowed = at >= first
            if distance == 0:
                allowed &= at <= lax.broadcasted_iota(jnp.int32, (count, RROWS), 1)
            scores = jnp.where(allowed, scores, -jnp.inf)
        peak = jnp.maximum(peak, jnp.max(scores, axis=0, keepdims=True))
        exps[rows] = scores
    total = jnp.zeros((1, RROWS), jnp.float32)
    for begin, count, _ in chunks:
        rows = slice(begin, begin + count)
        raised = jnp.exp2(exps[rows] - peak)
        total = total + jnp.sum(raised, axis=0, keepdims=True)
        exps[rows] = raised
    scale = 1.0 / total
    dq_t = jnp.zeros((WIDTH, RROWS), jnp.float32)
    prompt_sums = []
    for begin, count, distance in chunks:
        rows = slice(begin, begin + count)
        probs = exps[rows] * scale
        value_dot = jnp.dot(values[rows], dout_t, preferred_element_type=jnp.float32)
        score_grad = (probs * (value_dot - delta)).astype(jnp.bfloat16)
        dk = jnp.dot(score_grad, queries, preferred_element_type=jnp.float32) * FACTOR
        dv = jnp.dot(probs.astype(jnp.bfloat16), dout, preferred_element_type=jnp.float32)
        dq_t = dq_t + lax.dot_general(
            keys[rows], score_grad, (((0,), (0,)), ((), ())), preferred_element_type=jnp.float32
        )
        if distance is None:
            pair = jnp.stack(
                [dk.reshape(PIECES, TILE // 2, WIDTH), dv.reshape(PIECES, TILE // 2, WIDTH)], axis=1
            )
            prompt_sums.append(pair.reshape(PIECES * TILE, WIDTH).astype(jnp.bfloat16))
            continue
        dk, dv = dk.astype(jnp.bfloat16), dv.astype(jnp.bfloat16)
        half = RROWS // 2
        wide = jnp.concatenate([dk[:half], dk[half:], dv[:half], dv[half:]], axis=1)
        split = swapped(wide, swap).astype(jnp.bfloat16)
        for head in range(HEADS):
            block = split[:, head * WIDTH : (head + 1) * WIDTH]
            if distance == 0:
                close[head, PIECES * TILE :] = block
            else:
                far[(place[0] + HOPS - distance) & (Y - 1), head] = block
    split = swapped(jnp.concatenate(prompt_sums, axis=1), swap).astype(jnp.bfloat16)
    for head in range(HEADS):
        close[head, : PIECES * TILE] = split[:, head * WIDTH : (head + 1) * WIDTH]
    dq[...] = (dq_t.T * FACTOR).astype(jnp.bfloat16)


def attention(place, q, o, do, start, prompt, near):
    half = jnp.bfloat16
    keys_total = PROMPT + (HOPS + 1) * RROWS
    return pl.pallas_call(
        attention_kernel,
        out_shape=(
            jax.ShapeDtypeStruct((RROWS, WIDTH), half),
            jax.ShapeDtypeStruct((HEADS, PIECES * TILE + PACKED, WIDTH), half),
            jax.ShapeDtypeStruct((Y, HEADS, PACKED, WIDTH), half),
        ),
        in_specs=[SMEM] + [VMEM] * (5 + HOPS + 1),
        out_specs=(VMEM, VMEM, VMEM),
        scratch_shapes=[
            pltpu.VMEM((keys_total, RROWS), jnp.float32),
            pltpu.VMEM((keys_total, WIDTH), half),
            pltpu.VMEM((keys_total, WIDTH), half),
        ],
        compiler_params=PARAMS,
        cost_estimate=pl.CostEstimate(
            flops=12 * keys_total * RROWS * WIDTH, bytes_accessed=6_000_000, transcendentals=keys_total * RROWS
        ),
        name="attention",
    )(place, q, o, do, start, prompt, *near)


def select(slots, pieces):
    return pl.pallas_call(
        select_kernel,
        out_shape=jax.ShapeDtypeStruct((PIECES, TILE, WIDTH), jnp.bfloat16),
        in_specs=[SMEM, VMEM],
        out_specs=VMEM,
        compiler_params=PARAMS,
        name="select",
    )(slots, pieces)


def place_pieces(slots, landed):
    return pl.pallas_call(
        place_kernel,
        out_shape=(
            jax.ShapeDtypeStruct((DP, TILE, WIDTH), jnp.bfloat16),
            jax.ShapeDtypeStruct((PACKED, WIDTH), jnp.float32),
        ),
        in_specs=[SMEM, VMEM],
        out_specs=(VMEM, VMEM),
        compiler_params=PARAMS,
        name="place",
    )(slots, landed)


def exchanged(blocks, axes):
    return lax.all_to_all(blocks, axes, split_axis=0, concat_axis=0, tiled=True)


def given_to_all(block, axes):
    count = lax.axis_size(axes)
    return exchanged(jnp.broadcast_to(block[None], (count,) + block.shape), axes)


def shifted(array, by):
    pairs = [(i, i + by) for i in range(DP) if 0 <= i + by < DP]
    return lax.ppermute(array, ("xlo", "z", "y"), pairs)


def body(prompt_kv, resp_kv, resp_query, resp_out, resp_dout, resp_lengths, prompt_owner):
    half = jnp.bfloat16
    xlo, z, y = lax.axis_index("xlo"), lax.axis_index("z"), lax.axis_index("y")
    own_index = (xlo * Z + z) * Y + y
    own_group = own_index // PIECES

    along_z = given_to_all(prompt_kv.reshape(TILE, WIDTH), "z")
    resp_full = lax.all_gather(resp_kv.transpose(0, 2, 1), "head", axis=1, tiled=True)
    near = [resp_full] + [shifted(resp_full, d) for d in range(1, HOPS + 1)]
    pieces = given_to_all(along_z.reshape(Z * TILE, WIDTH), ("xlo", "y")).reshape(DP, TILE, WIDTH)

    holder = jnp.arange(DP, dtype=jnp.int32)
    slot = ((holder // (Z * Y)) * Y + holder % Y) * Z + (holder // Y) % Z
    own_pieces = own_group * PIECES + jnp.arange(PIECES, dtype=jnp.int32)
    slots = jnp.sum(
        jnp.where(own_pieces[:, None] == prompt_owner[None, :], slot[None, :], 0), axis=1
    ).astype(jnp.int32)
    picked = select(slots, pieces).reshape(PIECES * TILE, WIDTH)
    prompt = lax.all_gather(picked, "head", axis=0, tiled=False)

    offset = (own_index % PIECES) * RROWS + jnp.arange(RROWS, dtype=jnp.int32)
    lengths = jnp.sum(
        jnp.where(jnp.arange(resp_lengths.shape[0])[:, None] == own_group, resp_lengths, 0), axis=0
    )
    count = lengths.shape[0]
    earlier = jnp.arange(count)[None, :] <= jnp.arange(count)[:, None]
    bounds = jnp.sum(jnp.where(earlier, lengths[None, :], 0), axis=1)
    begun = jnp.max(jnp.where(bounds[:, None] <= offset[None, :], bounds[:, None], 0), axis=0)
    start = (begun - (own_index % PIECES) * RROWS).astype(jnp.int32)[None, :]

    place = jnp.reshape(y, (1,)).astype(jnp.int32)
    query_grad, close, far = attention(
        place, resp_query, resp_out, resp_dout, start, prompt, near
    )

    landed = exchanged(close, "head")
    far_landed = exchanged(far.reshape(Y * HEADS, PACKED, WIDTH), ("y", "head"))
    spread, own_sum = place_pieces(slots, landed)
    by_column = exchanged(spread.reshape(XLO * Y, Z * TILE, WIDTH), ("xlo", "y"))
    column_sum = jnp.sum(by_column.astype(jnp.float32), axis=0).astype(half)
    by_z = exchanged(column_sum.reshape(Z, TILE, WIDTH), "z")
    prompt_grad = jnp.sum(by_z.astype(jnp.float32), axis=0).astype(half)

    sender_sums = far_landed.reshape(Y, HEADS, PACKED, WIDTH).astype(jnp.float32)
    after = (jnp.arange(Y) > y)[:, None, None, None]
    same_plane = jnp.sum(jnp.where(after, sender_sums, 0.0), axis=(0, 1))
    plane_before = jnp.sum(jnp.where(after, 0.0, sender_sums), axis=(0, 1)).astype(half)
    from_plane_after = shifted(plane_before, -Y).astype(jnp.float32)
    resp_total = (own_sum + same_plane + from_plane_after).astype(half)
    resp_grad = resp_total.reshape(PACKED, HEADS, PART).transpose(1, 0, 2).reshape(2, RROWS, PART)
    return query_grad, resp_grad, prompt_grad.reshape(2, PROWS, PART)


def solution(mesh):
    fine = Mesh(np.asarray(mesh.devices).reshape(XLO, Z, Y, HEADS), ("xlo", "z", "y", "head"))
    dp = ("xlo", "z", "y")
    in_specs = (
        P(None, dp, "head"),
        P(None, dp, "head"),
        P(dp, "head"),
        P(dp, "head"),
        P(dp, "head"),
        P(),
        P(),
    )
    out_specs = (P(dp, "head"), P(None, dp, "head"), P(None, dp, "head"))
    return jax.shard_map(body, mesh=fine, in_specs=in_specs, out_specs=out_specs, check_vma=False)
```

```python
import jax
import jax.numpy as jnp
import numpy as np
from jax import lax
from jax.experimental import pallas as pl
from jax.experimental.pallas import tpu as pltpu
from jax.sharding import Mesh
from jax.sharding import PartitionSpec as P

XLO, Z, Y, HEADS = 2, 16, 4, 4
PLANES = XLO * Z
DP = PLANES * Y
WIDTH = 128
PART = WIDTH // HEADS
PIECES = 32
PROWS = 32
TILE = 2 * PROWS * PART // WIDTH
RROWS = 384
HOPS = 4
PROMPT = PIECES * PROWS
QUARTER = PROMPT // HEADS
FACTOR = WIDTH**-0.5
LOG2E = 1.4426950408889634
VMEM = pl.BlockSpec(memory_space=pltpu.VMEM)
SMEM = pl.BlockSpec(memory_space=pltpu.SMEM)
PARAMS = pltpu.CompilerParams(vmem_limit_bytes=32 * 1024 * 1024)


def swap_matrix():
    shape = (HEADS * WIDTH, HEADS * WIDTH)
    row = lax.broadcasted_iota(jnp.int32, shape, 0)
    col = lax.broadcasted_iota(jnp.int32, shape, 1)
    target = ((row >> 5) & 3) * WIDTH + (row >> 7) * PART + (row & 31)
    return jnp.where(target == col, 1.0, 0.0).astype(jnp.bfloat16)


def swapped(rows, swap):
    return jnp.dot(rows, swap, preferred_element_type=jnp.float32)


def fan_kernel(place, shares, own, other1, other2, other3, fanned, near):
    for column in range(Y):
        fanned[column] = shares[...]
    for step, part in enumerate((own, other1, other2, other3)):
        near[place[0] ^ step] = part[...]


def select_kernel(slots, pieces, picked):
    for piece in range(PIECES):
        picked[piece * TILE : (piece + 1) * TILE] = pieces[slots[piece]]


def place_kernel(slots, landed, spread):
    spread[...] = jnp.zeros_like(spread)
    total = landed[0].astype(jnp.float32)
    for head in range(1, HEADS):
        total = total + landed[head].astype(jnp.float32)
    rounded = total.astype(jnp.bfloat16)
    for piece in range(PIECES):
        spread[slots[piece]] = rounded[piece * TILE : (piece + 1) * TILE]


def column_kernel(landed, total):
    held = landed[0].astype(jnp.float32)
    for column in range(1, Y):
        held = held + landed[column].astype(jnp.float32)
    total[...] = held.astype(total.dtype)


def combine_kernel(place, own, far1, far2, far3, far4, mine, out1, out2, out3, slots):
    total = own[...]
    for far in (far1, far2, far3, far4):
        total = total + far[...].astype(jnp.float32)
    turned = [total[kind].T.astype(jnp.bfloat16) for kind in range(2)]
    for head in range(HEADS):
        for kind in range(2):
            slots[head, kind * PART : (kind + 1) * PART] = turned[kind][head * PART : (head + 1) * PART]
    for step, out in enumerate((mine, out1, out2, out3)):
        out[...] = slots[place[0] ^ step]


def attention_kernel(
    q, o, do, start, gathered, near0, near1, near2, near3, near4, dq, close, own, far1, far2, far3, far4, exps, keys, values
):
    swap = swap_matrix()
    packed = jnp.concatenate([gathered[c, : PIECES * TILE] for c in range(HEADS)], axis=1)
    columns = swapped(packed, swap)
    for quarter in range(HEADS):
        part = columns[:, quarter * WIDTH : (quarter + 1) * WIDTH].reshape(PIECES, 2, TILE // 2, WIDTH)
        rows = slice(quarter * QUARTER, (quarter + 1) * QUARTER)
        keys[rows] = part[:, 0].reshape(QUARTER, WIDTH).astype(jnp.bfloat16)
        values[rows] = part[:, 1].reshape(QUARTER, WIDTH).astype(jnp.bfloat16)
    for distance, near in enumerate((near0, near1, near2, near3, near4)):
        rows = slice(PROMPT + distance * RROWS, PROMPT + (distance + 1) * RROWS)
        for held, shift in ((keys, 0), (values, PART)):
            turned = [near[c, shift : shift + PART] for c in range(HEADS)]
            held[rows] = jnp.concatenate(turned, axis=0).T
    chunks = [(i * QUARTER, QUARTER, None) for i in range(HEADS)]
    chunks += [(PROMPT + d * RROWS, RROWS, d) for d in range(HOPS + 1)]
    queries, dout = q[...], do[...]
    queries_t, dout_t = queries.T, dout.T
    products = dout.astype(jnp.float32) * o[...].astype(jnp.float32)
    delta = jnp.sum(products.T, axis=0, keepdims=True)
    first = start[...]
    peak = jnp.full((1, RROWS), -jnp.inf, jnp.float32)
    for begin, count, distance in chunks:
        rows = slice(begin, begin + count)
        scores = jnp.dot(keys[rows], queries_t, preferred_element_type=jnp.float32) * (FACTOR * LOG2E)
        if distance is not None:
            at = lax.broadcasted_iota(jnp.int32, (count, RROWS), 0) - distance * RROWS
            allowed = at >= first
            if distance == 0:
                allowed &= at <= lax.broadcasted_iota(jnp.int32, (count, RROWS), 1)
            scores = jnp.where(allowed, scores, -jnp.inf)
        peak = jnp.maximum(peak, jnp.max(scores, axis=0, keepdims=True))
        exps[rows] = scores
    total = jnp.zeros((1, RROWS), jnp.float32)
    for begin, count, _ in chunks:
        rows = slice(begin, begin + count)
        raised = jnp.exp2(exps[rows] - peak)
        total = total + jnp.sum(raised, axis=0, keepdims=True)
        exps[rows] = raised
    scale = 1.0 / total
    dq_t = jnp.zeros((WIDTH, RROWS), jnp.float32)
    prompt_sums = []
    for begin, count, distance in chunks:
        rows = slice(begin, begin + count)
        probs = exps[rows] * scale
        value_dot = jnp.dot(values[rows], dout_t, preferred_element_type=jnp.float32)
        score_grad = (probs * (value_dot - delta)).astype(jnp.bfloat16)
        dk = jnp.dot(score_grad, queries, preferred_element_type=jnp.float32) * FACTOR
        dv = jnp.dot(probs.astype(jnp.bfloat16), dout, preferred_element_type=jnp.float32)
        dq_t = dq_t + lax.dot_general(
            keys[rows], score_grad, (((0,), (0,)), ((), ())), preferred_element_type=jnp.float32
        )
        if distance is None:
            pair = jnp.stack(
                [dk.reshape(PIECES, TILE // 2, WIDTH), dv.reshape(PIECES, TILE // 2, WIDTH)], axis=1
            )
            prompt_sums.append(pair.reshape(PIECES * TILE, WIDTH).astype(jnp.bfloat16))
            continue
        out = (own, far1, far2, far3, far4)[distance]
        out[0] = dk.astype(out.dtype)
        out[1] = dv.astype(out.dtype)
    split = swapped(jnp.concatenate(prompt_sums, axis=1), swap).astype(jnp.bfloat16)
    for head in range(HEADS):
        close[head] = split[:, head * WIDTH : (head + 1) * WIDTH]
    dq[...] = (dq_t.T * FACTOR).astype(jnp.bfloat16)


def local_call(kernel, name, shapes, operands, scratch=(), cost=None):
    scalars = sum(operand.ndim == 1 for operand in operands)
    arrays = len(operands) - scalars
    return pl.pallas_call(
        kernel,
        out_shape=[jax.ShapeDtypeStruct(shape, dtype) for shape, dtype in shapes],
        in_specs=[SMEM] * scalars + [VMEM] * arrays,
        out_specs=[VMEM] * len(shapes),
        scratch_shapes=scratch,
        compiler_params=PARAMS,
        cost_estimate=cost,
        name=name,
    )(*operands)


def attention(q, o, do, start, gathered, near):
    half = jnp.bfloat16
    total = PROMPT + (HOPS + 1) * RROWS
    block = (2, RROWS, WIDTH)
    shapes = [((RROWS, WIDTH), half), ((HEADS, PIECES * TILE, WIDTH), half), (block, jnp.float32)]
    return local_call(
        attention_kernel,
        "attention",
        shapes + [(block, half)] * HOPS,
        (q, o, do, start, gathered, *near),
        [
            pltpu.VMEM((total, RROWS), jnp.float32),
            pltpu.VMEM((total, WIDTH), half),
            pltpu.VMEM((total, WIDTH), half),
        ],
        pl.CostEstimate(
            flops=12 * total * RROWS * WIDTH, bytes_accessed=6_000_000, transcendentals=total * RROWS
        ),
    )


def exchanged(blocks, axes):
    return lax.all_to_all(blocks, axes, split_axis=0, concat_axis=0, tiled=True)


def given_to_all(block, axes):
    count = lax.axis_size(axes)
    return exchanged(jnp.broadcast_to(block[None], (count,) + block.shape), axes)


def shifted(array, by):
    pairs = [(i, i + by) for i in range(DP) if 0 <= i + by < DP]
    return lax.ppermute(array, ("xlo", "z", "y"), pairs)


def swapped_heads(array, step):
    return lax.ppermute(array, "head", [(i, i ^ step) for i in range(HEADS)])


def body(prompt_kv, resp_kv, resp_query, resp_out, resp_dout, resp_lengths, prompt_owner):
    half = jnp.bfloat16
    xlo, z, y = lax.axis_index("xlo"), lax.axis_index("z"), lax.axis_index("y")
    own_index = (xlo * Z + z) * Y + y
    own_group = own_index // PIECES

    head = lax.axis_index("head")
    place = head.reshape(1).astype(jnp.int32)
    own = resp_kv.transpose(0, 2, 1).reshape(2 * PART, RROWS)
    along_planes = given_to_all(prompt_kv.reshape(TILE, WIDTH), ("xlo", "z")).reshape(PLANES * TILE, WIDTH)
    fanned, near = local_call(
        fan_kernel,
        "fan",
        [((Y, PLANES * TILE, WIDTH), half), ((HEADS, 2 * PART, RROWS), half)],
        (place, along_planes, own, *[swapped_heads(own, step) for step in range(1, HEADS)]),
    )
    pieces = exchanged(fanned, "y").reshape(DP, TILE, WIDTH)
    near = [near] + [shifted(near, distance) for distance in range(1, HOPS + 1)]

    holder = jnp.arange(DP, dtype=jnp.int32)
    slot = (holder % Y) * PLANES + holder // Y
    own_pieces = own_group * PIECES + jnp.arange(PIECES, dtype=jnp.int32)
    owned = own_pieces[:, None] == prompt_owner[None, :]
    slots = jnp.sum(jnp.where(owned, slot[None, :], 0), axis=1).astype(jnp.int32)
    picked = local_call(select_kernel, "select", [((PIECES * TILE, WIDTH), half)], (slots, pieces))[0]
    gathered = lax.all_gather(picked, "head", axis=0, tiled=False)

    offset = (own_index % PIECES) * RROWS + jnp.arange(RROWS, dtype=jnp.int32)
    lengths = jnp.sum(
        jnp.where(jnp.arange(resp_lengths.shape[0])[:, None] == own_group, resp_lengths, 0), axis=0
    )
    count = lengths.shape[0]
    earlier = jnp.arange(count)[None, :] <= jnp.arange(count)[:, None]
    bounds = jnp.sum(jnp.where(earlier, lengths[None, :], 0), axis=1)
    begun = jnp.max(jnp.where(bounds[:, None] <= offset[None, :], bounds[:, None], 0), axis=0)
    start = (begun - (own_index % PIECES) * RROWS).astype(jnp.int32)[None, :]

    query_grad, close, own_terms, *fars = attention(
        resp_query, resp_out, resp_dout, start, gathered, near
    )

    landed = exchanged(close, "head")
    spread = local_call(place_kernel, "place", [((DP, TILE, WIDTH), half)], (slots, landed))[0]
    by_column = exchanged(spread.reshape(Y, PLANES * TILE, WIDTH), "y")
    column_sum = local_call(column_kernel, "column", [((PLANES * TILE, WIDTH), half)], (by_column,))[0]
    by_plane = exchanged(column_sum.reshape(PLANES, TILE, WIDTH), ("xlo", "z"))
    prompt_grad = jnp.sum(by_plane.astype(jnp.float32), axis=0).astype(half)

    fars = [shifted(far, -distance) for distance, far in enumerate(fars, 1)]
    cut = (2 * PART, RROWS)
    mine, *others = local_call(
        combine_kernel,
        "combine",
        [(cut, half)] * HEADS,
        (place, own_terms, *fars),
        [pltpu.VMEM((HEADS,) + cut, half)],
    )
    resp_total = mine.astype(jnp.float32)
    for step, other in enumerate(others, 1):
        resp_total = resp_total + swapped_heads(other, step).astype(jnp.float32)
    resp_grad = resp_total.astype(half).reshape(2, PART, RROWS).transpose(0, 2, 1)
    return query_grad, resp_grad, prompt_grad.reshape(2, PROWS, PART)


def solution(mesh):
    fine = Mesh(np.asarray(mesh.devices).reshape(XLO, Z, Y, HEADS), ("xlo", "z", "y", "head"))
    dp = ("xlo", "z", "y")
    in_specs = (
        P(None, dp, "head"),
        P(None, dp, "head"),
        P(dp, "head"),
        P(dp, "head"),
        P(dp, "head"),
        P(),
        P(),
    )
    out_specs = (P(dp, "head"), P(None, dp, "head"), P(None, dp, "head"))
    return jax.shard_map(body, mesh=fine, in_specs=in_specs, out_specs=out_specs, check_vma=False)
```

```python
import jax
import jax.numpy as jnp
import numpy as np
from jax import lax
from jax.experimental import pallas as pl
from jax.experimental.pallas import tpu as pltpu
from jax.sharding import Mesh
from jax.sharding import PartitionSpec as P

XLO, Z, Y, HEADS = 2, 16, 4, 4
DP = XLO * Z * Y
WIDTH = 128
PART = WIDTH // HEADS
PIECES = 32
PROWS = 32
TILE = 2 * PROWS * PART // WIDTH
RROWS = 384
HOPS = 4
PROMPT = PIECES * PROWS
QUARTER = PROMPT // HEADS
FACTOR = WIDTH**-0.5
LOG2E = 1.4426950408889634
VMEM = pl.BlockSpec(memory_space=pltpu.VMEM)
SMEM = pl.BlockSpec(memory_space=pltpu.SMEM)
PARAMS = pltpu.CompilerParams(vmem_limit_bytes=32 * 1024 * 1024)


def swap_matrix():
    shape = (HEADS * WIDTH, HEADS * WIDTH)
    row = lax.broadcasted_iota(jnp.int32, shape, 0)
    col = lax.broadcasted_iota(jnp.int32, shape, 1)
    target = ((row >> 5) & 3) * WIDTH + (row >> 7) * PART + (row & 31)
    return jnp.where(target == col, 1.0, 0.0).astype(jnp.bfloat16)


def swapped(rows, swap):
    return jnp.dot(rows, swap, preferred_element_type=jnp.float32)


def fan_kernel(shares, own, fanned, near):
    for column in range(XLO * Y):
        fanned[column] = shares[...]
    near[...] = own[...]


def select_kernel(slots, pieces, picked):
    for piece in range(PIECES):
        picked[piece * TILE : (piece + 1) * TILE] = pieces[slots[piece]]


def place_kernel(slots, landed, own, far2, far4, spread, partial):
    spread[...] = jnp.zeros_like(spread)
    total = landed[0].astype(jnp.float32)
    for head in range(1, HEADS):
        total = total + landed[head].astype(jnp.float32)
    rounded = total.astype(jnp.bfloat16)
    for piece in range(PIECES):
        spread[slots[piece]] = rounded[piece * TILE : (piece + 1) * TILE]
    partial[...] = own[...] + far2[...].astype(jnp.float32) + far4[...].astype(jnp.float32)


def column_kernel(place, landed, partial, far1, far3, column, mine, out1, out2, out3, slots):
    held = landed[0].astype(jnp.float32)
    for sender in range(1, XLO * Y):
        held = held + landed[sender].astype(jnp.float32)
    column[...] = held
    total = partial[...] + far1[...].astype(jnp.float32) + far3[...].astype(jnp.float32)
    turned = [total[kind].T.astype(jnp.bfloat16) for kind in range(2)]
    for head in range(HEADS):
        for kind in range(2):
            slots[head, kind * PART : (kind + 1) * PART] = turned[kind][head * PART : (head + 1) * PART]
    for step, out in enumerate((mine, out1, out2, out3)):
        out[...] = slots[place[0] ^ step]


def attention_kernel(
    q, o, do, start, gathered, near0, near1, near2, near3, near4, dq, close, own, far1, far2, far3, far4, exps, keys, values
):
    swap = swap_matrix()
    packed = jnp.concatenate([gathered[c, : PIECES * TILE] for c in range(HEADS)], axis=1)
    columns = swapped(packed, swap)
    for quarter in range(HEADS):
        part = columns[:, quarter * WIDTH : (quarter + 1) * WIDTH].reshape(PIECES, 2, TILE // 2, WIDTH)
        rows = slice(quarter * QUARTER, (quarter + 1) * QUARTER)
        keys[rows] = part[:, 0].reshape(QUARTER, WIDTH).astype(jnp.bfloat16)
        values[rows] = part[:, 1].reshape(QUARTER, WIDTH).astype(jnp.bfloat16)
    for distance, near in enumerate((near0, near1, near2, near3, near4)):
        rows = slice(PROMPT + distance * RROWS, PROMPT + (distance + 1) * RROWS)
        keys[rows] = near[0].T
        values[rows] = near[1].T
    chunks = [(i * QUARTER, QUARTER, None) for i in range(HEADS)]
    chunks += [(PROMPT + d * RROWS, RROWS, d) for d in range(HOPS + 1)]
    queries, dout = q[...], do[...]
    queries_t, dout_t = queries.T, dout.T
    products = dout.astype(jnp.float32) * o[...].astype(jnp.float32)
    delta = jnp.sum(products.T, axis=0, keepdims=True)
    first = start[...]
    peak = jnp.full((1, RROWS), -jnp.inf, jnp.float32)
    for begin, count, distance in chunks:
        rows = slice(begin, begin + count)
        scores = jnp.dot(keys[rows], queries_t, preferred_element_type=jnp.float32) * (FACTOR * LOG2E)
        if distance is not None:
            at = lax.broadcasted_iota(jnp.int32, (count, RROWS), 0) - distance * RROWS
            allowed = at >= first
            if distance == 0:
                allowed &= at <= lax.broadcasted_iota(jnp.int32, (count, RROWS), 1)
            scores = jnp.where(allowed, scores, -jnp.inf)
        peak = jnp.maximum(peak, jnp.max(scores, axis=0, keepdims=True))
        exps[rows] = scores
    total = jnp.zeros((1, RROWS), jnp.float32)
    for begin, count, _ in chunks:
        rows = slice(begin, begin + count)
        raised = jnp.exp2(exps[rows] - peak)
        total = total + jnp.sum(raised, axis=0, keepdims=True)
        exps[rows] = raised
    scale = 1.0 / total
    dq_t = jnp.zeros((WIDTH, RROWS), jnp.float32)
    prompt_sums = []
    for begin, count, distance in chunks:
        rows = slice(begin, begin + count)
        probs = exps[rows] * scale
        value_dot = jnp.dot(values[rows], dout_t, preferred_element_type=jnp.float32)
        score_grad = (probs * (value_dot - delta)).astype(jnp.bfloat16)
        dk = jnp.dot(score_grad, queries, preferred_element_type=jnp.float32) * FACTOR
        dv = jnp.dot(probs.astype(jnp.bfloat16), dout, preferred_element_type=jnp.float32)
        dq_t = dq_t + lax.dot_general(
            keys[rows], score_grad, (((0,), (0,)), ((), ())), preferred_element_type=jnp.float32
        )
        if distance is None:
            pair = jnp.stack(
                [dk.reshape(PIECES, TILE // 2, WIDTH), dv.reshape(PIECES, TILE // 2, WIDTH)], axis=1
            )
            prompt_sums.append(pair.reshape(PIECES * TILE, WIDTH).astype(jnp.bfloat16))
            continue
        out = (own, far1, far2, far3, far4)[distance]
        out[0] = dk.astype(out.dtype)
        out[1] = dv.astype(out.dtype)
    split = swapped(jnp.concatenate(prompt_sums, axis=1), swap).astype(jnp.bfloat16)
    for head in range(HEADS):
        close[head] = split[:, head * WIDTH : (head + 1) * WIDTH]
    dq[...] = (dq_t.T * FACTOR).astype(jnp.bfloat16)


def local_call(kernel, name, shapes, operands, scratch=(), cost=None):
    scalars = sum(operand.ndim == 1 for operand in operands)
    arrays = len(operands) - scalars
    return pl.pallas_call(
        kernel,
        out_shape=[jax.ShapeDtypeStruct(shape, dtype) for shape, dtype in shapes],
        in_specs=[SMEM] * scalars + [VMEM] * arrays,
        out_specs=[VMEM] * len(shapes),
        scratch_shapes=scratch,
        compiler_params=PARAMS,
        cost_estimate=cost,
        name=name,
    )(*operands)


def attention(q, o, do, start, gathered, near):
    half = jnp.bfloat16
    total = PROMPT + (HOPS + 1) * RROWS
    block = (2, RROWS, WIDTH)
    shapes = [((RROWS, WIDTH), half), ((HEADS, PIECES * TILE, WIDTH), half), (block, jnp.float32)]
    return local_call(
        attention_kernel,
        "attention",
        shapes + [(block, half)] * HOPS,
        (q, o, do, start, gathered, *near),
        [
            pltpu.VMEM((total, RROWS), jnp.float32),
            pltpu.VMEM((total, WIDTH), half),
            pltpu.VMEM((total, WIDTH), half),
        ],
        pl.CostEstimate(
            flops=12 * total * RROWS * WIDTH, bytes_accessed=6_000_000, transcendentals=total * RROWS
        ),
    )


def exchanged(blocks, axes):
    return lax.all_to_all(blocks, axes, split_axis=0, concat_axis=0, tiled=True)


def given_to_all(block, axes):
    count = lax.axis_size(axes)
    return exchanged(jnp.broadcast_to(block[None], (count,) + block.shape), axes)


def shifted(array, by):
    pairs = [(i, i + by) for i in range(DP) if 0 <= i + by < DP]
    return lax.ppermute(array, ("xlo", "z", "y"), pairs)


def swapped_heads(array, step):
    return lax.ppermute(array, "head", [(i, i ^ step) for i in range(HEADS)])


def body(prompt_kv, resp_kv, resp_query, resp_out, resp_dout, resp_lengths, prompt_owner):
    half = jnp.bfloat16
    xlo, z, y = lax.axis_index("xlo"), lax.axis_index("z"), lax.axis_index("y")
    own_index = (xlo * Z + z) * Y + y
    own_group = own_index // PIECES

    head = lax.axis_index("head")
    place = head.reshape(1).astype(jnp.int32)
    own = lax.all_gather(resp_kv.transpose(0, 2, 1), "head", axis=1, tiled=True)
    along_z = given_to_all(prompt_kv.reshape(TILE, WIDTH), "z").reshape(Z * TILE, WIDTH)
    fanned, near = local_call(
        fan_kernel,
        "fan",
        [((XLO * Y, Z * TILE, WIDTH), half), ((2, WIDTH, RROWS), half)],
        (along_z, own),
    )
    pieces = exchanged(fanned, ("xlo", "y")).reshape(DP, TILE, WIDTH)
    near = [near] + [shifted(near, distance) for distance in range(1, HOPS + 1)]

    holder = jnp.arange(DP, dtype=jnp.int32)
    slot = ((holder // (Z * Y)) * Y + holder % Y) * Z + (holder // Y) % Z
    own_pieces = own_group * PIECES + jnp.arange(PIECES, dtype=jnp.int32)
    owned = own_pieces[:, None] == prompt_owner[None, :]
    slots = jnp.sum(jnp.where(owned, slot[None, :], 0), axis=1).astype(jnp.int32)
    picked = local_call(select_kernel, "select", [((PIECES * TILE, WIDTH), half)], (slots, pieces))[0]
    gathered = lax.all_gather(picked, "head", axis=0, tiled=False)

    offset = (own_index % PIECES) * RROWS + jnp.arange(RROWS, dtype=jnp.int32)
    lengths = jnp.sum(
        jnp.where(jnp.arange(resp_lengths.shape[0])[:, None] == own_group, resp_lengths, 0), axis=0
    )
    count = lengths.shape[0]
    earlier = jnp.arange(count)[None, :] <= jnp.arange(count)[:, None]
    bounds = jnp.sum(jnp.where(earlier, lengths[None, :], 0), axis=1)
    begun = jnp.max(jnp.where(bounds[:, None] <= offset[None, :], bounds[:, None], 0), axis=0)
    start = (begun - (own_index % PIECES) * RROWS).astype(jnp.int32)[None, :]

    query_grad, close, own_terms, *fars = attention(
        resp_query, resp_out, resp_dout, start, gathered, near
    )

    landed = exchanged(close, "head")
    fars = [shifted(far, -distance) for distance, far in enumerate(fars, 1)]
    spread, partial = local_call(
        place_kernel,
        "place",
        [((DP, TILE, WIDTH), half), ((2, RROWS, WIDTH), jnp.float32)],
        (slots, landed, own_terms, fars[1], fars[3]),
    )
    by_column = exchanged(spread.reshape(XLO * Y, Z * TILE, WIDTH), ("xlo", "y"))
    cut = (2 * PART, RROWS)
    column_sum, mine, *others = local_call(
        column_kernel,
        "column",
        [((Z * TILE, WIDTH), jnp.float32)] + [(cut, half)] * HEADS,
        (place, by_column, partial, fars[0], fars[2]),
        [pltpu.VMEM((HEADS,) + cut, half)],
    )
    by_z = exchanged(column_sum.reshape(Z, TILE, WIDTH), "z")
    prompt_grad = jnp.sum(by_z, axis=0).astype(half)

    resp_total = mine.astype(jnp.float32)
    for step, other in enumerate(others, 1):
        resp_total = resp_total + swapped_heads(other, step).astype(jnp.float32)
    resp_grad = resp_total.astype(half).reshape(2, PART, RROWS).transpose(0, 2, 1)
    return query_grad, resp_grad, prompt_grad.reshape(2, PROWS, PART)


def solution(mesh):
    fine = Mesh(np.asarray(mesh.devices).reshape(XLO, Z, Y, HEADS), ("xlo", "z", "y", "head"))
    dp = ("xlo", "z", "y")
    in_specs = (
        P(None, dp, "head"),
        P(None, dp, "head"),
        P(dp, "head"),
        P(dp, "head"),
        P(dp, "head"),
        P(),
        P(),
    )
    out_specs = (P(dp, "head"), P(None, dp, "head"), P(None, dp, "head"))
    return jax.shard_map(body, mesh=fine, in_specs=in_specs, out_specs=out_specs, check_vma=False)
```

```python
import jax
import jax.numpy as jnp
import numpy as np
from jax import lax
from jax.experimental import pallas as pl
from jax.experimental.pallas import tpu as pltpu
from jax.sharding import Mesh
from jax.sharding import PartitionSpec as P

XLO, Z, Y, XHI, CORES = 2, 16, 4, 2, 2
HEADS = XHI * CORES
DP = XLO * Z * Y
COLUMNS = XLO * Y
WIDTH = 128
PART = WIDTH // HEADS
PIECES = 32
PROWS = 32
TILE = 2 * PROWS * PART // WIDTH
RROWS = 384
HOPS = 4
PROMPT = PIECES * PROWS
QUARTER = PROMPT // HEADS
FACTOR = WIDTH**-0.5
LOG2E = 1.4426950408889634
VMEM = pl.BlockSpec(memory_space=pltpu.VMEM)
SMEM = pl.BlockSpec(memory_space=pltpu.SMEM)
PARAMS = pltpu.CompilerParams(vmem_limit_bytes=32 * 1024 * 1024)


def swap_matrix():
    shape = (HEADS * WIDTH, HEADS * WIDTH)
    row = lax.broadcasted_iota(jnp.int32, shape, 0)
    col = lax.broadcasted_iota(jnp.int32, shape, 1)
    target = ((row >> 5) & 3) * WIDTH + (row >> 7) * PART + (row & 31)
    return jnp.where(target == col, 1.0, 0.0).astype(jnp.bfloat16)


def swapped(rows, swap):
    return jnp.dot(rows, swap, preferred_element_type=jnp.float32)


def fan_kernel(shares, own, fanned, near):
    for column in range(COLUMNS):
        fanned[column] = shares[...]
    near[...] = own[...]


def select_kernel(slots, pieces, picked):
    for piece in range(PIECES):
        picked[piece * TILE : (piece + 1) * TILE] = pieces[slots[piece]]


def pair_kernel(place, kept, kept_near, landed, mine, other, own, far1, far23, far4, cut):
    for xhi in range(XHI):
        theirs = landed[xhi * PIECES * TILE : (xhi + 1) * PIECES * TILE]
        cut[xhi] = kept[xhi].astype(jnp.float32) + theirs.astype(jnp.float32)
    mine[...] = cut[place[1]]
    other[...] = cut[1 - place[1]].astype(other.dtype)
    for distance, (out, at) in enumerate(((own, 0), (far1, 0), (far23, 0), (far23, WIDTH), (far4, 0))):
        for column in range(RROWS // WIDTH):
            lanes = slice(column * WIDTH, (column + 1) * WIDTH)
            theirs = landed[near_row(distance, column) : near_row(distance, column) + WIDTH]
            out[at : at + WIDTH, lanes] = (kept_near[distance, :, lanes] + theirs.astype(jnp.float32)).astype(out.dtype)


def place_kernel(slots, mine, theirs, own, far1, far23, far4, spread, partial, passed):
    spread[...] = jnp.zeros_like(spread)
    total = (mine[...] + theirs[...].astype(jnp.float32)).astype(jnp.bfloat16)
    for piece in range(PIECES):
        spread[slots[piece]] = total[piece * TILE : (piece + 1) * TILE]
    partial[...] = own[...] + far23[:WIDTH].astype(jnp.float32) + far4[...].astype(jnp.float32)
    passed[...] = (far1[...].astype(jnp.float32) + far23[WIDTH:].astype(jnp.float32)).astype(passed.dtype)


def near_row(distance, column):
    return XHI * PIECES * TILE + (distance * (RROWS // WIDTH) + column) * WIDTH


def column_kernel(place, landed, partial, passed, column, mine, other, cut):
    held = landed[0].astype(jnp.float32)
    for sender in range(1, COLUMNS):
        held = held + landed[sender].astype(jnp.float32)
    column[...] = held
    total = partial[...] + passed[...].astype(jnp.float32)
    for xhi in range(XHI):
        for kind in range(2):
            begin = (kind * XHI + xhi) * PART
            cut[xhi, kind * PART : (kind + 1) * PART] = total[begin : begin + PART]
    mine[...] = cut[place[1]]
    other[...] = cut[1 - place[1]].astype(other.dtype)


def attention_kernel(
    place, q, o, do, start, gathered, near0, near1, near23, near4,
    dq, kept, kept_near, sent, exps, keys, values, heads, turned,
):
    swap = swap_matrix()
    core = place[0]
    packed = jnp.concatenate([gathered[c] for c in range(HEADS)], axis=1)
    columns = swapped(packed, swap)
    for quarter in range(HEADS):
        part = columns[:, quarter * WIDTH : (quarter + 1) * WIDTH].reshape(PIECES, 2, TILE // 2, WIDTH)
        rows = slice(quarter * QUARTER, (quarter + 1) * QUARTER)
        keys[rows] = part[:, 0].reshape(QUARTER, WIDTH).astype(jnp.bfloat16)
        values[rows] = part[:, 1].reshape(QUARTER, WIDTH).astype(jnp.bfloat16)
    for distance, (near, at) in enumerate(((near0, 0), (near1, 0), (near23, 0), (near23, 2), (near4, 0))):
        rows = slice(PROMPT + distance * RROWS, PROMPT + (distance + 1) * RROWS)
        keys[rows] = near[at].T
        values[rows] = near[at + 1].T
    chunks = [(i * QUARTER, QUARTER, None) for i in range(HEADS)]
    chunks += [(PROMPT + d * RROWS, RROWS, d) for d in range(HOPS + 1)]
    queries, dout = q[...], do[...]
    queries_t, dout_t = queries.T, dout.T
    products = dout.astype(jnp.float32) * o[...].astype(jnp.float32)
    delta = jnp.sum(products.T, axis=0, keepdims=True)
    first = start[...]
    peak = jnp.full((1, RROWS), -jnp.inf, jnp.float32)
    for begin, count, distance in chunks:
        rows = slice(begin, begin + count)
        scores = jnp.dot(keys[rows], queries_t, preferred_element_type=jnp.float32) * (FACTOR * LOG2E)
        if distance is not None:
            at = lax.broadcasted_iota(jnp.int32, (count, RROWS), 0) - distance * RROWS
            allowed = at >= first
            if distance == 0:
                allowed &= at <= lax.broadcasted_iota(jnp.int32, (count, RROWS), 1)
            scores = jnp.where(allowed, scores, -jnp.inf)
        peak = jnp.maximum(peak, jnp.max(scores, axis=0, keepdims=True))
        exps[rows] = scores
    total = jnp.zeros((1, RROWS), jnp.float32)
    for begin, count, _ in chunks:
        rows = slice(begin, begin + count)
        raised = jnp.exp2(exps[rows] - peak)
        total = total + jnp.sum(raised, axis=0, keepdims=True)
        exps[rows] = raised
    scale = 1.0 / total
    dq_t = jnp.zeros((WIDTH, RROWS), jnp.float32)
    prompt_sums = []
    for begin, count, distance in chunks:
        rows = slice(begin, begin + count)
        probs = exps[rows] * scale
        value_dot = jnp.dot(values[rows], dout_t, preferred_element_type=jnp.float32)
        score_grad = (probs * (value_dot - delta)).astype(jnp.bfloat16)
        dk = jnp.dot(score_grad, queries, preferred_element_type=jnp.float32) * FACTOR
        dv = jnp.dot(probs.astype(jnp.bfloat16), dout, preferred_element_type=jnp.float32)
        dq_t = dq_t + lax.dot_general(
            keys[rows], score_grad, (((0,), (0,)), ((), ())), preferred_element_type=jnp.float32
        )
        if distance is None:
            pair = jnp.stack(
                [dk.reshape(PIECES, TILE // 2, WIDTH), dv.reshape(PIECES, TILE // 2, WIDTH)], axis=1
            )
            prompt_sums.append(pair.reshape(PIECES * TILE, WIDTH).astype(jnp.bfloat16))
            continue
        for kind, terms in enumerate((dk, dv)):
            turned[distance, kind] = terms.T
            for xhi in range(XHI):
                rows = slice((kind * XHI + xhi) * PART, (kind * XHI + xhi + 1) * PART)
                at = pl.multiple_of((xhi * CORES + core) * PART, PART)
                kept_near[distance, rows] = turned[distance, kind, pl.ds(at, PART)]
                at = pl.multiple_of((xhi * CORES + 1 - core) * PART, PART)
                leaving = turned[distance, kind, pl.ds(at, PART)].astype(jnp.bfloat16)
                for column in range(RROWS // WIDTH):
                    first_row = near_row(distance, column)
                    sent[first_row + rows.start : first_row + rows.stop] = leaving[
                        :, column * WIDTH : (column + 1) * WIDTH
                    ]
    split = swapped(jnp.concatenate(prompt_sums, axis=1), swap).astype(jnp.bfloat16)
    for head in range(HEADS):
        heads[head] = split[:, head * WIDTH : (head + 1) * WIDTH]
    for xhi in range(XHI):
        kept[xhi] = heads[xhi * CORES + core]
        sent[xhi * PIECES * TILE : (xhi + 1) * PIECES * TILE] = heads[xhi * CORES + 1 - core]
    dq[...] = (dq_t.T * FACTOR).astype(jnp.bfloat16)


def local_call(kernel, name, shapes, operands, scratch=(), cost=None):
    scalars = sum(operand.ndim == 1 for operand in operands)
    arrays = len(operands) - scalars
    return pl.pallas_call(
        kernel,
        out_shape=[jax.ShapeDtypeStruct(shape, dtype) for shape, dtype in shapes],
        in_specs=[SMEM] * scalars + [VMEM] * arrays,
        out_specs=[VMEM] * len(shapes),
        scratch_shapes=scratch,
        compiler_params=PARAMS,
        cost_estimate=cost,
        name=name,
    )(*operands)


def attention(place, q, o, do, start, gathered, near):
    half = jnp.bfloat16
    total = PROMPT + (HOPS + 1) * RROWS
    return local_call(
        attention_kernel,
        "attention",
        [
            ((RROWS, WIDTH), half),
            ((XHI, PIECES * TILE, WIDTH), half),
            ((HOPS + 1, 2 * XHI * PART, RROWS), jnp.float32),
            ((near_row(HOPS + 1, 0), WIDTH), half),
        ],
        (place, q, o, do, start, gathered, *near),
        [
            pltpu.VMEM((total, RROWS), jnp.float32),
            pltpu.VMEM((total, WIDTH), half),
            pltpu.VMEM((total, WIDTH), half),
            pltpu.VMEM((HEADS, PIECES * TILE, WIDTH), half),
            pltpu.VMEM((HOPS + 1, 2, WIDTH, RROWS), jnp.float32),
        ],
        pl.CostEstimate(
            flops=12 * total * RROWS * WIDTH, bytes_accessed=6_000_000, transcendentals=total * RROWS
        ),
    )


def exchanged(blocks, axes):
    return lax.all_to_all(blocks, axes, split_axis=0, concat_axis=0, tiled=True)


def given_to_all(block, axes):
    count = lax.axis_size(axes)
    return exchanged(jnp.broadcast_to(block[None], (count,) + block.shape), axes)


def shifted(array, by):
    pairs = [(i, i + by) for i in range(DP) if 0 <= i + by < DP]
    return lax.ppermute(array, ("xlo", "z", "y"), pairs)


def traded(array, axis):
    return lax.ppermute(array, axis, [(0, 1), (1, 0)])


def body(prompt_kv, resp_kv, resp_query, resp_out, resp_dout, resp_lengths, prompt_owner):
    half = jnp.bfloat16
    xlo, z, y = lax.axis_index("xlo"), lax.axis_index("z"), lax.axis_index("y")
    own_index = (xlo * Z + z) * Y + y
    own_group = own_index // PIECES

    place = jnp.stack([lax.axis_index("core"), lax.axis_index("xhi")]).astype(jnp.int32)
    own = lax.all_gather(resp_kv.transpose(0, 2, 1), ("xhi", "core"), axis=1, tiled=True)
    along_z = given_to_all(prompt_kv.reshape(TILE, WIDTH), "z").reshape(Z * TILE, WIDTH)
    fanned, near = local_call(
        fan_kernel,
        "fan",
        [((COLUMNS, Z * TILE, WIDTH), half), ((2, WIDTH, RROWS), half)],
        (along_z, own),
    )
    pieces = exchanged(fanned, ("xlo", "y")).reshape(DP, TILE, WIDTH)
    near1, near4 = shifted(near, 1), shifted(near, HOPS)
    near23 = shifted(jnp.concatenate([near, near1], axis=0), 2)
    near = [near, near1, near23, near4]

    holder = jnp.arange(DP, dtype=jnp.int32)
    slot = ((holder // (Z * Y)) * Y + holder % Y) * Z + (holder // Y) % Z
    own_pieces = own_group * PIECES + jnp.arange(PIECES, dtype=jnp.int32)
    owned = own_pieces[:, None] == prompt_owner[None, :]
    slots = jnp.sum(jnp.where(owned, slot[None, :], 0), axis=1).astype(jnp.int32)
    picked = local_call(select_kernel, "select", [((PIECES * TILE, WIDTH), half)], (slots, pieces))[0]
    gathered = lax.all_gather(picked, ("xhi", "core"), axis=0, tiled=False)

    offset = (own_index % PIECES) * RROWS + jnp.arange(RROWS, dtype=jnp.int32)
    lengths = jnp.sum(
        jnp.where(jnp.arange(resp_lengths.shape[0])[:, None] == own_group, resp_lengths, 0), axis=0
    )
    count = lengths.shape[0]
    earlier = jnp.arange(count)[None, :] <= jnp.arange(count)[:, None]
    bounds = jnp.sum(jnp.where(earlier, lengths[None, :], 0), axis=1)
    begun = jnp.max(jnp.where(bounds[:, None] <= offset[None, :], bounds[:, None], 0), axis=0)
    start = (begun - (own_index % PIECES) * RROWS).astype(jnp.int32)[None, :]

    query_grad, kept, kept_near, sent = attention(
        place, resp_query, resp_out, resp_dout, start, gathered, near
    )

    pieces_shape, wide, narrow = (PIECES * TILE, WIDTH), (2 * XHI * PART, RROWS), (2 * PART, RROWS)
    mine, other, own_terms, far1, far23, far4 = local_call(
        pair_kernel,
        "pair",
        [(pieces_shape, jnp.float32), (pieces_shape, half), (wide, jnp.float32)]
        + [(wide, half), ((2 * wide[0], RROWS), half), (wide, half)],
        (place, kept, kept_near, traded(sent, "core")),
        [pltpu.VMEM((XHI,) + pieces_shape, jnp.float32)],
    )
    theirs = traded(other, "xhi")
    spread, partial, passed = local_call(
        place_kernel,
        "place",
        [((DP, TILE, WIDTH), half), (wide, jnp.float32), (wide, half)],
        (slots, mine, theirs, own_terms, far1, shifted(far23, -2), shifted(far4, -HOPS)),
    )
    by_column = exchanged(spread.reshape(COLUMNS, Z * TILE, WIDTH), ("xlo", "y"))
    column_sum, mine, other = local_call(
        column_kernel,
        "column",
        [((Z * TILE, WIDTH), jnp.float32), (narrow, jnp.float32), (narrow, half)],
        (place, by_column, partial, shifted(passed, -1)),
        [pltpu.VMEM((XHI,) + narrow, jnp.float32)],
    )
    by_z = exchanged(column_sum.reshape(Z, TILE, WIDTH), "z")
    prompt_grad = jnp.sum(by_z, axis=0).astype(half)

    resp_total = mine + traded(other, "xhi").astype(jnp.float32)
    resp_grad = resp_total.astype(half).reshape(2, PART, RROWS).transpose(0, 2, 1)
    return query_grad, resp_grad, prompt_grad.reshape(2, PROWS, PART)


def solution(mesh):
    fine = Mesh(np.asarray(mesh.devices).reshape(XLO, Z, Y, XHI, CORES), ("xlo", "z", "y", "xhi", "core"))
    dp, head = ("xlo", "z", "y"), ("xhi", "core")
    in_specs = (
        P(None, dp, head),
        P(None, dp, head),
        P(dp, head),
        P(dp, head),
        P(dp, head),
        P(),
        P(),
    )
    out_specs = (P(dp, head), P(None, dp, head), P(None, dp, head))
    return jax.shard_map(body, mesh=fine, in_specs=in_specs, out_specs=out_specs, check_vma=False)
```

```python
import jax
import jax.numpy as jnp
import numpy as np
from jax import lax
from jax.experimental import pallas as pl
from jax.experimental.pallas import tpu as pltpu
from jax.sharding import Mesh
from jax.sharding import PartitionSpec as P

XLO, Z, Y, XHI, CORES = 2, 16, 4, 2, 2
HEADS = XHI * CORES
DP = XLO * Z * Y
COLUMNS = XLO * Y
WIDTH = 128
PART = WIDTH // HEADS
PIECES = 32
PROWS = 32
TILE = 2 * PROWS * PART // WIDTH
RROWS = 384
HOPS = 4
PROMPT = PIECES * PROWS
QUARTER = PROMPT // HEADS
FACTOR = WIDTH**-0.5
LOG2E = 1.4426950408889634
VMEM = pl.BlockSpec(memory_space=pltpu.VMEM)
SMEM = pl.BlockSpec(memory_space=pltpu.SMEM)
PARAMS = pltpu.CompilerParams(vmem_limit_bytes=32 * 1024 * 1024)


def swap_matrix():
    shape = (HEADS * WIDTH, HEADS * WIDTH)
    row = lax.broadcasted_iota(jnp.int32, shape, 0)
    col = lax.broadcasted_iota(jnp.int32, shape, 1)
    target = ((row >> 5) & 3) * WIDTH + (row >> 7) * PART + (row & 31)
    return jnp.where(target == col, 1.0, 0.0).astype(jnp.bfloat16)


def swapped(rows, swap):
    return jnp.dot(rows, swap, preferred_element_type=jnp.float32)


def fan_kernel(shares, own, fanned, near):
    for column in range(COLUMNS):
        fanned[column] = shares[...]
    near[...] = own[...]


def select_kernel(slots, pieces, picked):
    for piece in range(PIECES):
        picked[piece * TILE : (piece + 1) * TILE] = pieces[slots[piece]]


def pair_kernel(place, kept, kept_near, landed, mine, other, own, far1, far23, far4, cut):
    for xhi in range(XHI):
        theirs = landed[xhi * PIECES * TILE : (xhi + 1) * PIECES * TILE]
        cut[xhi] = kept[xhi].astype(jnp.float32) + theirs.astype(jnp.float32)
    mine[...] = cut[place[1]]
    other[...] = cut[1 - place[1]].astype(other.dtype)
    for distance, (out, at) in enumerate(((own, 0), (far1, 0), (far23, 0), (far23, WIDTH), (far4, 0))):
        for column in range(RROWS // WIDTH):
            lanes = slice(column * WIDTH, (column + 1) * WIDTH)
            theirs = landed[near_row(distance, column) : near_row(distance, column) + WIDTH]
            out[at : at + WIDTH, lanes] = (kept_near[distance, :, lanes] + theirs.astype(jnp.float32)).astype(out.dtype)


def place_kernel(slots, mine, theirs, own, far1, far23, far4, spread, partial, passed):
    spread[...] = jnp.zeros_like(spread)
    total = (mine[...] + theirs[...].astype(jnp.float32)).astype(jnp.bfloat16)
    for piece in range(PIECES):
        spread[slots[piece]] = total[piece * TILE : (piece + 1) * TILE]
    partial[...] = own[...] + far23[:WIDTH].astype(jnp.float32) + far4[...].astype(jnp.float32)
    passed[...] = (far1[...].astype(jnp.float32) + far23[WIDTH:].astype(jnp.float32)).astype(passed.dtype)


def near_row(distance, column):
    return XHI * PIECES * TILE + (distance * (RROWS // WIDTH) + column) * WIDTH


def column_kernel(place, landed, partial, passed, column, mine, other, cut):
    held = landed[0].astype(jnp.float32)
    for sender in range(1, COLUMNS):
        held = held + landed[sender].astype(jnp.float32)
    column[...] = held
    total = partial[...] + passed[...].astype(jnp.float32)
    for xhi in range(XHI):
        for kind in range(2):
            begin = (kind * XHI + xhi) * PART
            cut[xhi, kind * PART : (kind + 1) * PART] = total[begin : begin + PART]
    mine[...] = cut[place[1]]
    other[...] = cut[1 - place[1]].astype(other.dtype)


def attention_kernel(
    place, q, o, do, start, gathered, near0, near1, near2, near3, near4,
    dq, kept, kept_near, sent, exps, keys, values, heads, turned,
):
    swap = swap_matrix()
    core = place[0]
    packed = jnp.concatenate([gathered[c] for c in range(HEADS)], axis=1)
    columns = swapped(packed, swap)
    for quarter in range(HEADS):
        part = columns[:, quarter * WIDTH : (quarter + 1) * WIDTH].reshape(PIECES, 2, TILE // 2, WIDTH)
        rows = slice(quarter * QUARTER, (quarter + 1) * QUARTER)
        keys[rows] = part[:, 0].reshape(QUARTER, WIDTH).astype(jnp.bfloat16)
        values[rows] = part[:, 1].reshape(QUARTER, WIDTH).astype(jnp.bfloat16)
    for distance, near in enumerate((near0, near1, near2, near3, near4)):
        rows = slice(PROMPT + distance * RROWS, PROMPT + (distance + 1) * RROWS)
        keys[rows] = near[0].T
        values[rows] = near[1].T
    chunks = [(i * QUARTER, QUARTER, None) for i in range(HEADS)]
    chunks += [(PROMPT + d * RROWS, RROWS, d) for d in range(HOPS + 1)]
    queries, dout = q[...], do[...]
    queries_t, dout_t = queries.T, dout.T
    products = dout.astype(jnp.float32) * o[...].astype(jnp.float32)
    delta = jnp.sum(products.T, axis=0, keepdims=True)
    first = start[...]
    peak = jnp.full((1, RROWS), -jnp.inf, jnp.float32)
    for begin, count, distance in chunks:
        rows = slice(begin, begin + count)
        scores = jnp.dot(keys[rows], queries_t, preferred_element_type=jnp.float32) * (FACTOR * LOG2E)
        if distance is not None:
            at = lax.broadcasted_iota(jnp.int32, (count, RROWS), 0) - distance * RROWS
            allowed = at >= first
            if distance == 0:
                allowed &= at <= lax.broadcasted_iota(jnp.int32, (count, RROWS), 1)
            scores = jnp.where(allowed, scores, -jnp.inf)
        peak = jnp.maximum(peak, jnp.max(scores, axis=0, keepdims=True))
        exps[rows] = scores
    total = jnp.zeros((1, RROWS), jnp.float32)
    for begin, count, _ in chunks:
        rows = slice(begin, begin + count)
        raised = jnp.exp2(exps[rows] - peak)
        total = total + jnp.sum(raised, axis=0, keepdims=True)
        exps[rows] = raised
    scale = 1.0 / total
    dq_t = jnp.zeros((WIDTH, RROWS), jnp.float32)
    prompt_sums = []
    for begin, count, distance in chunks:
        rows = slice(begin, begin + count)
        probs = exps[rows] * scale
        value_dot = jnp.dot(values[rows], dout_t, preferred_element_type=jnp.float32)
        score_grad = (probs * (value_dot - delta)).astype(jnp.bfloat16)
        dk = jnp.dot(score_grad, queries, preferred_element_type=jnp.float32) * FACTOR
        dv = jnp.dot(probs.astype(jnp.bfloat16), dout, preferred_element_type=jnp.float32)
        dq_t = dq_t + lax.dot_general(
            keys[rows], score_grad, (((0,), (0,)), ((), ())), preferred_element_type=jnp.float32
        )
        if distance is None:
            pair = jnp.stack(
                [dk.reshape(PIECES, TILE // 2, WIDTH), dv.reshape(PIECES, TILE // 2, WIDTH)], axis=1
            )
            prompt_sums.append(pair.reshape(PIECES * TILE, WIDTH).astype(jnp.bfloat16))
            continue
        for kind, terms in enumerate((dk, dv)):
            turned[distance, kind] = terms.T
            for xhi in range(XHI):
                rows = slice((kind * XHI + xhi) * PART, (kind * XHI + xhi + 1) * PART)
                at = pl.multiple_of((xhi * CORES + core) * PART, PART)
                kept_near[distance, rows] = turned[distance, kind, pl.ds(at, PART)]
                at = pl.multiple_of((xhi * CORES + 1 - core) * PART, PART)
                leaving = turned[distance, kind, pl.ds(at, PART)].astype(jnp.bfloat16)
                for column in range(RROWS // WIDTH):
                    first_row = near_row(distance, column)
                    sent[first_row + rows.start : first_row + rows.stop] = leaving[
                        :, column * WIDTH : (column + 1) * WIDTH
                    ]
    split = swapped(jnp.concatenate(prompt_sums, axis=1), swap).astype(jnp.bfloat16)
    for head in range(HEADS):
        heads[head] = split[:, head * WIDTH : (head + 1) * WIDTH]
    for xhi in range(XHI):
        kept[xhi] = heads[xhi * CORES + core]
        sent[xhi * PIECES * TILE : (xhi + 1) * PIECES * TILE] = heads[xhi * CORES + 1 - core]
    dq[...] = (dq_t.T * FACTOR).astype(jnp.bfloat16)


def local_call(kernel, name, shapes, operands, scratch=(), cost=None):
    scalars = sum(operand.ndim == 1 for operand in operands)
    arrays = len(operands) - scalars
    return pl.pallas_call(
        kernel,
        out_shape=[jax.ShapeDtypeStruct(shape, dtype) for shape, dtype in shapes],
        in_specs=[SMEM] * scalars + [VMEM] * arrays,
        out_specs=[VMEM] * len(shapes),
        scratch_shapes=scratch,
        compiler_params=PARAMS,
        cost_estimate=cost,
        name=name,
    )(*operands)


def attention(place, q, o, do, start, gathered, near):
    half = jnp.bfloat16
    total = PROMPT + (HOPS + 1) * RROWS
    return local_call(
        attention_kernel,
        "attention",
        [
            ((RROWS, WIDTH), half),
            ((XHI, PIECES * TILE, WIDTH), half),
            ((HOPS + 1, 2 * XHI * PART, RROWS), jnp.float32),
            ((near_row(HOPS + 1, 0), WIDTH), half),
        ],
        (place, q, o, do, start, gathered, *near),
        [
            pltpu.VMEM((total, RROWS), jnp.float32),
            pltpu.VMEM((total, WIDTH), half),
            pltpu.VMEM((total, WIDTH), half),
            pltpu.VMEM((HEADS, PIECES * TILE, WIDTH), half),
            pltpu.VMEM((HOPS + 1, 2, WIDTH, RROWS), jnp.float32),
        ],
        pl.CostEstimate(
            flops=12 * total * RROWS * WIDTH, bytes_accessed=6_000_000, transcendentals=total * RROWS
        ),
    )


def exchanged(blocks, axes):
    return lax.all_to_all(blocks, axes, split_axis=0, concat_axis=0, tiled=True)


def given_to_all(block, axes):
    count = lax.axis_size(axes)
    return exchanged(jnp.broadcast_to(block[None], (count,) + block.shape), axes)


def shifted(array, by):
    pairs = [(i, i + by) for i in range(DP) if i // PIECES == (i + by) // PIECES]
    return lax.ppermute(array, ("xlo", "z", "y"), pairs)


def traded(array, axis):
    return lax.ppermute(array, axis, [(0, 1), (1, 0)])


def body(prompt_kv, resp_kv, resp_query, resp_out, resp_dout, resp_lengths, prompt_owner):
    half = jnp.bfloat16
    xlo, z, y = lax.axis_index("xlo"), lax.axis_index("z"), lax.axis_index("y")
    own_index = (xlo * Z + z) * Y + y
    own_group = own_index // PIECES

    place = jnp.stack([lax.axis_index("core"), lax.axis_index("xhi")]).astype(jnp.int32)
    own = lax.all_gather(resp_kv.transpose(0, 2, 1), ("xhi", "core"), axis=1, tiled=True)
    along_z = given_to_all(prompt_kv.reshape(TILE, WIDTH), "z").reshape(Z * TILE, WIDTH)
    fanned, near = local_call(
        fan_kernel,
        "fan",
        [((COLUMNS, Z * TILE, WIDTH), half), ((2, WIDTH, RROWS), half)],
        (along_z, own),
    )
    pieces = exchanged(fanned, ("xlo", "y")).reshape(DP, TILE, WIDTH)
    near = [near] + [shifted(near, distance) for distance in range(1, HOPS + 1)]

    holder = jnp.arange(DP, dtype=jnp.int32)
    slot = ((holder // (Z * Y)) * Y + holder % Y) * Z + (holder // Y) % Z
    own_pieces = own_group * PIECES + jnp.arange(PIECES, dtype=jnp.int32)
    owned = own_pieces[:, None] == prompt_owner[None, :]
    slots = jnp.sum(jnp.where(owned, slot[None, :], 0), axis=1).astype(jnp.int32)
    picked = local_call(select_kernel, "select", [((PIECES * TILE, WIDTH), half)], (slots, pieces))[0]
    gathered = lax.all_gather(picked, ("xhi", "core"), axis=0, tiled=False)

    offset = (own_index % PIECES) * RROWS + jnp.arange(RROWS, dtype=jnp.int32)
    lengths = jnp.sum(
        jnp.where(jnp.arange(resp_lengths.shape[0])[:, None] == own_group, resp_lengths, 0), axis=0
    )
    count = lengths.shape[0]
    earlier = jnp.arange(count)[None, :] <= jnp.arange(count)[:, None]
    bounds = jnp.sum(jnp.where(earlier, lengths[None, :], 0), axis=1)
    begun = jnp.max(jnp.where(bounds[:, None] <= offset[None, :], bounds[:, None], 0), axis=0)
    start = (begun - (own_index % PIECES) * RROWS).astype(jnp.int32)[None, :]

    query_grad, kept, kept_near, sent = attention(
        place, resp_query, resp_out, resp_dout, start, gathered, near
    )

    pieces_shape, wide, narrow = (PIECES * TILE, WIDTH), (2 * XHI * PART, RROWS), (2 * PART, RROWS)
    mine, other, own_terms, far1, far23, far4 = local_call(
        pair_kernel,
        "pair",
        [(pieces_shape, jnp.float32), (pieces_shape, half), (wide, jnp.float32)]
        + [(wide, half), ((2 * wide[0], RROWS), half), (wide, half)],
        (place, kept, kept_near, traded(sent, "core")),
        [pltpu.VMEM((XHI,) + pieces_shape, jnp.float32)],
    )
    theirs = traded(other, "xhi")
    spread, partial, passed = local_call(
        place_kernel,
        "place",
        [((DP, TILE, WIDTH), half), (wide, jnp.float32), (wide, half)],
        (slots, mine, theirs, own_terms, far1, shifted(far23, -2), shifted(far4, -HOPS)),
    )
    by_column = exchanged(spread.reshape(COLUMNS, Z * TILE, WIDTH), ("xlo", "y"))
    column_sum, mine, other = local_call(
        column_kernel,
        "column",
        [((Z * TILE, WIDTH), jnp.float32), (narrow, jnp.float32), (narrow, half)],
        (place, by_column, partial, shifted(passed, -1)),
        [pltpu.VMEM((XHI,) + narrow, jnp.float32)],
    )
    by_z = exchanged(column_sum.reshape(Z, TILE, WIDTH), "z")
    prompt_grad = jnp.sum(by_z, axis=0).astype(half)

    resp_total = mine + traded(other, "xhi").astype(jnp.float32)
    resp_grad = resp_total.astype(half).reshape(2, PART, RROWS).transpose(0, 2, 1)
    return query_grad, resp_grad, prompt_grad.reshape(2, PROWS, PART)


def solution(mesh):
    fine = Mesh(np.asarray(mesh.devices).reshape(XLO, Z, Y, XHI, CORES), ("xlo", "z", "y", "xhi", "core"))
    dp, head = ("xlo", "z", "y"), ("xhi", "core")
    in_specs = (
        P(None, dp, head),
        P(None, dp, head),
        P(dp, head),
        P(dp, head),
        P(dp, head),
        P(),
        P(),
    )
    out_specs = (P(dp, head), P(None, dp, head), P(None, dp, head))
    return jax.shard_map(body, mesh=fine, in_specs=in_specs, out_specs=out_specs, check_vma=False)
```

```python
import jax
import jax.numpy as jnp
import numpy as np
from jax import lax
from jax.experimental import pallas as pl
from jax.experimental.pallas import tpu as pltpu
from jax.sharding import Mesh
from jax.sharding import PartitionSpec as P

XLO, Z, Y, XHI, CORES = 2, 16, 4, 2, 2
HEADS = XHI * CORES
DP = XLO * Z * Y
COLUMNS = XLO * Y
WIDTH = 128
PART = WIDTH // HEADS
PIECES = 32
PROWS = 32
TILE = 2 * PROWS * PART // WIDTH
RROWS = 384
HOPS = 4
PROMPT = PIECES * PROWS
QUARTER = PROMPT // HEADS
FACTOR = WIDTH**-0.5
LOG2E = 1.4426950408889634
VMEM = pl.BlockSpec(memory_space=pltpu.VMEM)
SMEM = pl.BlockSpec(memory_space=pltpu.SMEM)
PARAMS = pltpu.CompilerParams(vmem_limit_bytes=32 * 1024 * 1024)


def swap_matrix():
    shape = (HEADS * WIDTH, HEADS * WIDTH)
    row = lax.broadcasted_iota(jnp.int32, shape, 0)
    col = lax.broadcasted_iota(jnp.int32, shape, 1)
    target = ((row >> 5) & 3) * WIDTH + (row >> 7) * PART + (row & 31)
    return jnp.where(target == col, 1.0, 0.0).astype(jnp.bfloat16)


def swapped(rows, swap):
    return jnp.dot(rows, swap, preferred_element_type=jnp.float32)


def fan_kernel(shares, own, fanned, near):
    for column in range(COLUMNS):
        fanned[column] = shares[...]
    near[...] = own[...]


def select_kernel(slots, pieces, picked):
    for piece in range(PIECES):
        picked[piece * TILE : (piece + 1) * TILE] = pieces[slots[piece]]


def pair_kernel(place, kept, kept_near, landed, mine, other, own, far1, far23, far4, cut):
    for xhi in range(XHI):
        theirs = landed[xhi * PIECES * TILE : (xhi + 1) * PIECES * TILE]
        cut[xhi] = kept[xhi].astype(jnp.float32) + theirs.astype(jnp.float32)
    mine[...] = cut[place[1]]
    other[...] = cut[1 - place[1]].astype(other.dtype)
    for distance, (out, at) in enumerate(((own, 0), (far1, 0), (far23, 0), (far23, WIDTH), (far4, 0))):
        for column in range(RROWS // WIDTH):
            lanes = slice(column * WIDTH, (column + 1) * WIDTH)
            theirs = landed[near_row(distance, column) : near_row(distance, column) + WIDTH]
            out[at : at + WIDTH, lanes] = (kept_near[distance, :, lanes] + theirs.astype(jnp.float32)).astype(out.dtype)


def place_kernel(slots, mine, theirs, own, far1, far23, spread, partial, passed):
    spread[...] = jnp.zeros_like(spread)
    total = (mine[...] + theirs[...].astype(jnp.float32)).astype(jnp.bfloat16)
    for piece in range(PIECES):
        spread[slots[piece]] = total[piece * TILE : (piece + 1) * TILE]
    partial[...] = own[...] + far23[:WIDTH].astype(jnp.float32)
    passed[...] = (far1[...].astype(jnp.float32) + far23[WIDTH:].astype(jnp.float32)).astype(passed.dtype)


def near_row(distance, column):
    return XHI * PIECES * TILE + (distance * (RROWS // WIDTH) + column) * WIDTH


def column_kernel(place, landed, partial, passed, far4, column, mine, other, cut):
    held = landed[0].astype(jnp.float32)
    for sender in range(1, COLUMNS):
        held = held + landed[sender].astype(jnp.float32)
    column[...] = held
    total = partial[...] + passed[...].astype(jnp.float32) + far4[...].astype(jnp.float32)
    for xhi in range(XHI):
        for kind in range(2):
            begin = (kind * XHI + xhi) * PART
            cut[xhi, kind * PART : (kind + 1) * PART] = total[begin : begin + PART]
    mine[...] = cut[place[1]]
    other[...] = cut[1 - place[1]].astype(other.dtype)


def attention_kernel(
    place, q, o, do, start, gathered, near0, near1, near2, near3, near4,
    dq, kept, kept_near, sent, exps, keys, values, heads, turned,
):
    swap = swap_matrix()
    core = place[0]
    packed = jnp.concatenate([gathered[c] for c in range(HEADS)], axis=1)
    columns = swapped(packed, swap)
    for quarter in range(HEADS):
        part = columns[:, quarter * WIDTH : (quarter + 1) * WIDTH].reshape(PIECES, 2, TILE // 2, WIDTH)
        rows = slice(quarter * QUARTER, (quarter + 1) * QUARTER)
        keys[rows] = part[:, 0].reshape(QUARTER, WIDTH).astype(jnp.bfloat16)
        values[rows] = part[:, 1].reshape(QUARTER, WIDTH).astype(jnp.bfloat16)
    for distance, near in enumerate((near0, near1, near2, near3, near4)):
        rows = slice(PROMPT + distance * RROWS, PROMPT + (distance + 1) * RROWS)
        keys[rows] = near[0].T
        values[rows] = near[1].T
    chunks = [(i * QUARTER, QUARTER, None) for i in range(HEADS)]
    chunks += [(PROMPT + d * RROWS, RROWS, d) for d in range(HOPS + 1)]
    queries, dout = q[...], do[...]
    queries_t, dout_t = queries.T, dout.T
    products = dout.astype(jnp.float32) * o[...].astype(jnp.float32)
    delta = jnp.sum(products.T, axis=0, keepdims=True)
    first = start[...]
    peak = jnp.full((1, RROWS), -jnp.inf, jnp.float32)
    for begin, count, distance in chunks:
        rows = slice(begin, begin + count)
        scores = jnp.dot(keys[rows], queries_t, preferred_element_type=jnp.float32) * (FACTOR * LOG2E)
        if distance is not None:
            at = lax.broadcasted_iota(jnp.int32, (count, RROWS), 0) - distance * RROWS
            allowed = at >= first
            if distance == 0:
                allowed &= at <= lax.broadcasted_iota(jnp.int32, (count, RROWS), 1)
            scores = jnp.where(allowed, scores, -jnp.inf)
        peak = jnp.maximum(peak, jnp.max(scores, axis=0, keepdims=True))
        exps[rows] = scores
    total = jnp.zeros((1, RROWS), jnp.float32)
    for begin, count, _ in chunks:
        rows = slice(begin, begin + count)
        raised = jnp.exp2(exps[rows] - peak)
        total = total + jnp.sum(raised, axis=0, keepdims=True)
        exps[rows] = raised
    scale = 1.0 / total
    dq_t = jnp.zeros((WIDTH, RROWS), jnp.float32)
    prompt_sums = []
    for begin, count, distance in chunks:
        rows = slice(begin, begin + count)
        probs = exps[rows] * scale
        value_dot = jnp.dot(values[rows], dout_t, preferred_element_type=jnp.float32)
        score_grad = (probs * (value_dot - delta)).astype(jnp.bfloat16)
        dk = jnp.dot(score_grad, queries, preferred_element_type=jnp.float32) * FACTOR
        dv = jnp.dot(probs.astype(jnp.bfloat16), dout, preferred_element_type=jnp.float32)
        dq_t = dq_t + lax.dot_general(
            keys[rows], score_grad, (((0,), (0,)), ((), ())), preferred_element_type=jnp.float32
        )
        if distance is None:
            pair = jnp.stack(
                [dk.reshape(PIECES, TILE // 2, WIDTH), dv.reshape(PIECES, TILE // 2, WIDTH)], axis=1
            )
            prompt_sums.append(pair.reshape(PIECES * TILE, WIDTH).astype(jnp.bfloat16))
            continue
        for kind, terms in enumerate((dk, dv)):
            turned[distance, kind] = terms.T
            for xhi in range(XHI):
                rows = slice((kind * XHI + xhi) * PART, (kind * XHI + xhi + 1) * PART)
                at = pl.multiple_of((xhi * CORES + core) * PART, PART)
                kept_near[distance, rows] = turned[distance, kind, pl.ds(at, PART)]
                at = pl.multiple_of((xhi * CORES + 1 - core) * PART, PART)
                leaving = turned[distance, kind, pl.ds(at, PART)].astype(jnp.bfloat16)
                for column in range(RROWS // WIDTH):
                    first_row = near_row(distance, column)
                    sent[first_row + rows.start : first_row + rows.stop] = leaving[
                        :, column * WIDTH : (column + 1) * WIDTH
                    ]
    split = swapped(jnp.concatenate(prompt_sums, axis=1), swap).astype(jnp.bfloat16)
    for head in range(HEADS):
        heads[head] = split[:, head * WIDTH : (head + 1) * WIDTH]
    for xhi in range(XHI):
        kept[xhi] = heads[xhi * CORES + core]
        sent[xhi * PIECES * TILE : (xhi + 1) * PIECES * TILE] = heads[xhi * CORES + 1 - core]
    dq[...] = (dq_t.T * FACTOR).astype(jnp.bfloat16)


def local_call(kernel, name, shapes, operands, scratch=(), cost=None):
    scalars = sum(operand.ndim == 1 for operand in operands)
    arrays = len(operands) - scalars
    return pl.pallas_call(
        kernel,
        out_shape=[jax.ShapeDtypeStruct(shape, dtype) for shape, dtype in shapes],
        in_specs=[SMEM] * scalars + [VMEM] * arrays,
        out_specs=[VMEM] * len(shapes),
        scratch_shapes=scratch,
        compiler_params=PARAMS,
        cost_estimate=cost,
        name=name,
    )(*operands)


def attention(place, q, o, do, start, gathered, near):
    half = jnp.bfloat16
    total = PROMPT + (HOPS + 1) * RROWS
    return local_call(
        attention_kernel,
        "attention",
        [
            ((RROWS, WIDTH), half),
            ((XHI, PIECES * TILE, WIDTH), half),
            ((HOPS + 1, 2 * XHI * PART, RROWS), jnp.float32),
            ((near_row(HOPS + 1, 0), WIDTH), half),
        ],
        (place, q, o, do, start, gathered, *near),
        [
            pltpu.VMEM((total, RROWS), jnp.float32),
            pltpu.VMEM((total, WIDTH), half),
            pltpu.VMEM((total, WIDTH), half),
            pltpu.VMEM((HEADS, PIECES * TILE, WIDTH), half),
            pltpu.VMEM((HOPS + 1, 2, WIDTH, RROWS), jnp.float32),
        ],
        pl.CostEstimate(
            flops=12 * total * RROWS * WIDTH, bytes_accessed=6_000_000, transcendentals=total * RROWS
        ),
    )


def exchanged(blocks, axes):
    return lax.all_to_all(blocks, axes, split_axis=0, concat_axis=0, tiled=True)


def given_to_all(block, axes):
    count = lax.axis_size(axes)
    return exchanged(jnp.broadcast_to(block[None], (count,) + block.shape), axes)


def shifted(array, by):
    pairs = [(i, i + by) for i in range(DP) if i // PIECES == (i + by) // PIECES]
    return lax.ppermute(array, ("xlo", "z", "y"), pairs)


def traded(array, axis):
    return lax.ppermute(array, axis, [(0, 1), (1, 0)])


def body(prompt_kv, resp_kv, resp_query, resp_out, resp_dout, resp_lengths, prompt_owner):
    half = jnp.bfloat16
    xlo, z, y = lax.axis_index("xlo"), lax.axis_index("z"), lax.axis_index("y")
    own_index = (xlo * Z + z) * Y + y
    own_group = own_index // PIECES

    place = jnp.stack([lax.axis_index("core"), lax.axis_index("xhi")]).astype(jnp.int32)
    own = lax.all_gather(resp_kv.transpose(0, 2, 1), ("xhi", "core"), axis=1, tiled=True)
    along_z = given_to_all(prompt_kv.reshape(TILE, WIDTH), "z").reshape(Z * TILE, WIDTH)
    fanned, near = local_call(
        fan_kernel,
        "fan",
        [((COLUMNS, Z * TILE, WIDTH), half), ((2, WIDTH, RROWS), half)],
        (along_z, own),
    )
    pieces = exchanged(fanned, ("xlo", "y")).reshape(DP, TILE, WIDTH)
    near = [near] + [shifted(near, distance) for distance in range(1, HOPS + 1)]

    holder = jnp.arange(DP, dtype=jnp.int32)
    slot = ((holder // (Z * Y)) * Y + holder % Y) * Z + (holder // Y) % Z
    own_pieces = own_group * PIECES + jnp.arange(PIECES, dtype=jnp.int32)
    owned = own_pieces[:, None] == prompt_owner[None, :]
    slots = jnp.sum(jnp.where(owned, slot[None, :], 0), axis=1).astype(jnp.int32)
    picked = local_call(select_kernel, "select", [((PIECES * TILE, WIDTH), half)], (slots, pieces))[0]
    gathered = lax.all_gather(picked, ("xhi", "core"), axis=0, tiled=False)

    offset = (own_index % PIECES) * RROWS + jnp.arange(RROWS, dtype=jnp.int32)
    lengths = jnp.sum(
        jnp.where(jnp.arange(resp_lengths.shape[0])[:, None] == own_group, resp_lengths, 0), axis=0
    )
    count = lengths.shape[0]
    earlier = jnp.arange(count)[None, :] <= jnp.arange(count)[:, None]
    bounds = jnp.sum(jnp.where(earlier, lengths[None, :], 0), axis=1)
    begun = jnp.max(jnp.where(bounds[:, None] <= offset[None, :], bounds[:, None], 0), axis=0)
    start = (begun - (own_index % PIECES) * RROWS).astype(jnp.int32)[None, :]

    query_grad, kept, kept_near, sent = attention(
        place, resp_query, resp_out, resp_dout, start, gathered, near
    )

    pieces_shape, wide, narrow = (PIECES * TILE, WIDTH), (2 * XHI * PART, RROWS), (2 * PART, RROWS)
    mine, other, own_terms, far1, far23, far4 = local_call(
        pair_kernel,
        "pair",
        [(pieces_shape, jnp.float32), (pieces_shape, half), (wide, jnp.float32)]
        + [(wide, half), ((2 * wide[0], RROWS), half), (wide, half)],
        (place, kept, kept_near, traded(sent, "core")),
        [pltpu.VMEM((XHI,) + pieces_shape, jnp.float32)],
    )
    theirs = traded(other, "xhi")
    spread, partial, passed = local_call(
        place_kernel,
        "place",
        [((DP, TILE, WIDTH), half), (wide, jnp.float32), (wide, half)],
        (slots, mine, theirs, own_terms, far1, shifted(far23, -2)),
    )
    by_column = exchanged(spread.reshape(COLUMNS, Z * TILE, WIDTH), ("xlo", "y"))
    column_sum, mine, other = local_call(
        column_kernel,
        "column",
        [((Z * TILE, WIDTH), jnp.float32), (narrow, jnp.float32), (narrow, half)],
        (place, by_column, partial, shifted(passed, -1), shifted(far4, -HOPS)),
        [pltpu.VMEM((XHI,) + narrow, jnp.float32)],
    )
    by_z = exchanged(column_sum.reshape(Z, TILE, WIDTH), "z")
    prompt_grad = jnp.sum(by_z, axis=0).astype(half)

    resp_total = mine + traded(other, "xhi").astype(jnp.float32)
    resp_grad = resp_total.astype(half).reshape(2, PART, RROWS).transpose(0, 2, 1)
    return query_grad, resp_grad, prompt_grad.reshape(2, PROWS, PART)


def solution(mesh):
    fine = Mesh(np.asarray(mesh.devices).reshape(XLO, Z, Y, XHI, CORES), ("xlo", "z", "y", "xhi", "core"))
    dp, head = ("xlo", "z", "y"), ("xhi", "core")
    in_specs = (
        P(None, dp, head),
        P(None, dp, head),
        P(dp, head),
        P(dp, head),
        P(dp, head),
        P(),
        P(),
    )
    out_specs = (P(dp, head), P(None, dp, head), P(None, dp, head))
    return jax.shard_map(body, mesh=fine, in_specs=in_specs, out_specs=out_specs, check_vma=False)
```
